32 devices in a mesh: tm: 4 (over z), row: 8 (over y, x, core).
Axes of the slice: x: 2, y: 2, z: 4, core: 2. Of those that a mesh axis runs over, the one named last changes fastest.
Arguments:
- visible: bfloat16 [4, 8, 8, 4, 1024], P('tm', 'row'), may hold values from -6 to 6
- slot_pos: int32 [4, 8, 8, 4], P('tm', 'row'), may hold values from -1 to 255, as said below
- window_shift: int32 [2, 2], replicated, may hold values from 0 to 3, as said below
- mask_token: bfloat16 [1024], replicated, may hold values from -6 to 6
- w_qkv: bfloat16 [1024, 3072], replicated, may hold values from -6.25 to 6.25
- w_out: bfloat16 [1024, 1024], replicated, may hold values from -0.1875 to 0.1875
- w_head: bfloat16 [1024, 1536], replicated, may hold values from -0.1875 to 0.1875
- pixels: bfloat16 [16, 32, 16, 1536], P('tm', 'row'), may hold values from 0 to 1
Outputs:
- d_visible: bfloat16 [4, 8, 8, 4, 1024], P('tm', 'row')
- d_mask_token: float32 [1024], replicated
The draws below stay inside these ranges and needn't reach their ends.
Inputs may be any that keep to these rules, and one draw needn't show every extreme that they name: Each live entry slot_pos[i, s, d, c] is a token index of decoder shard (i, d) in frame, row, column order; the live entries aimed at one shard (i, d) are distinct; every slot slot_pos[i, s, s, c] is live, so each shard receives all 4 slots from the packed shard of its own band; other slots are live or -1 at rates that differ from packed shard to packed shard. window_shift[0, g] lies in 0 to 1 and window_shift[1, g] in 0 to 3; some block of columns has row offset 4 - 1 and some block has frame offset 0.
All inputs are finite; a program needn't handle non-finite values.
Results may differ from the reference program's by a relative error of at most 0.014.
Values may be sent and summed in bfloat16 or wider, within the bound.
A program may use at most 128 MiB of HBM per device.

```python
import math
import jax
import jax.numpy as jnp
from jax import lax

D = 1024
HEADS = 16
PIX = 1536
WT = 2
WH = 4
WW = 8
CAP = 4
TL = 4
HL = 4
W = 16
NT = 16
NH = 32
TOKENS = 8192
N_TM = 4
N_ROW = 8


def draw_w_qkv(key, part):
    base = jnp.clip(jax.random.normal(key, (D, 3 * D), jnp.float32), -5.0, 5.0) * D ** (-0.5)
    return base.astype(jnp.bfloat16)


def draw_window_shift(key, part):
    group_count = W // WW
    frame_offsets = jax.random.randint(jax.random.fold_in(key, 31), (group_count,), 0, WT)
    row_offsets = jax.random.randint(jax.random.fold_in(key, 32), (group_count,), 0, WH)
    row_pick = jax.random.randint(jax.random.fold_in(key, 33), (), 0, group_count)
    frame_pick = jax.random.randint(jax.random.fold_in(key, 34), (), 0, group_count)
    group_ids = jnp.arange(group_count, dtype=jnp.int32)
    row_offsets = jnp.where(group_ids == row_pick, WH - 1, row_offsets)
    frame_offsets = jnp.where(group_ids == frame_pick, 0, frame_offsets)
    return jnp.stack([frame_offsets, row_offsets], axis=0).astype(jnp.int32)


def draw_slot_pos(key, part):
    tokens = TL * HL * W
    groups = N_TM * N_ROW

    def one_group(group_key):
        return jax.random.permutation(group_key, tokens)[:N_ROW * CAP]
    chosen = jax.vmap(one_group)(jax.random.split(key, groups)).reshape(N_TM, N_ROW, N_ROW, CAP)
    keep_rates = jax.random.randint(jax.random.fold_in(key, 11), (N_TM, 1, N_ROW, 1), 15, 66)
    roll_values = jax.random.randint(jax.random.fold_in(key, 12), (N_TM, N_ROW, N_ROW, CAP), 0, 100)
    same_peer = (jnp.arange(N_ROW)[:, None] == jnp.arange(N_ROW)[None, :])[None, :, :, None]
    is_live = (roll_values < keep_rates) | same_peer
    placed = jnp.where(is_live, chosen, -1)
    return jnp.transpose(placed, (0, 2, 1, 3)).astype(jnp.int32)


def levels(rng, dims, shards, least, largest):
    level = 1.0
    for axis_at, parts in shards:
        draws = jax.random.uniform(jax.random.fold_in(jax.random.fold_in(rng, 6), axis_at), (parts,), jnp.float32, least / len(shards), largest / len(shards))
        level = level * jnp.repeat(jnp.exp(draws), dims[axis_at] // parts).reshape((-1,) + (1,) * (len(dims) - 1 - axis_at))
    return level


def centred(stream_key, dims, deviation, limit, shards=(), kind=jnp.bfloat16):
    drawn = deviation * jax.random.normal(stream_key, dims, jnp.float32)
    if shards:
        drawn = drawn * levels(stream_key, dims, shards, -0.22, 0.18)
    return jnp.clip(drawn, -limit, limit).astype(kind)


def setup_inputs(seed: int = 0) -> dict:
    streams_of = jax.random.split(jax.random.key(seed), 9)
    return {
        "visible": centred(streams_of[0], (N_TM, N_ROW, N_ROW, CAP, D), 1.0, 6.0, ((0, 4), (1, 8))),
        "slot_pos": draw_slot_pos(jax.random.fold_in(streams_of[8], 71), 0),
        "window_shift": draw_window_shift(jax.random.fold_in(streams_of[8], 71), 0),
        "mask_token": centred(streams_of[3], (D,), 1.0, 6.0),
        "w_qkv": draw_w_qkv(jax.random.fold_in(streams_of[8], 71), 0),
        "w_out": centred(streams_of[5], (D, D), D ** -0.5, 0.1875),
        "w_head": centred(streams_of[6], (D, PIX), D ** -0.5, 0.1875),
        "pixels": jnp.clip(1.0 * jax.random.uniform(streams_of[7], (NT, NH, W, PIX), jnp.float32) ** levels(streams_of[7], (NT, NH, W, PIX), ((0, 4), (1, 8)), -0.2, 0.2), 0.0, 1.0).astype(jnp.bfloat16),
    }


def layer_norm(values):
    center = values - lax.optimization_barrier(jnp.mean(values, axis=-1, keepdims=True))
    return center * lax.rsqrt(lax.optimization_barrier(jnp.mean(center * center, axis=-1, keepdims=True)) + 1e-05)

def sinusoid(coordinate, channel_count):
    half_count = channel_count // 2
    frequency = jnp.exp(-math.log(10000.0) * jnp.arange(half_count, dtype=jnp.float32) / half_count)
    angles = coordinate.astype(jnp.float32)[..., None] * frequency
    return jnp.concatenate([jnp.sin(angles), jnp.cos(angles)], axis=-1)

def position_table(frame_pos, row_pos, column_pos, model_width):
    quarter = model_width // 4
    remainder = (model_width - quarter) // 2
    return jnp.concatenate([sinusoid(frame_pos, quarter), sinusoid(row_pos, remainder), sinusoid(column_pos, model_width - quarter - remainder)], axis=-1)

def window_core(grid_block, w_qkv, w_out):
    frame_count, row_count, column_count, model_width = grid_block.shape
    head_dim = model_width // HEADS
    normed = layer_norm(grid_block).astype(jnp.bfloat16)
    packed = jnp.dot(normed.reshape(-1, model_width), w_qkv, preferred_element_type=jnp.float32).astype(jnp.bfloat16)
    packed = packed.reshape(frame_count // WT, WT, row_count // WH, WH, column_count // WW, WW, 3, HEADS, head_dim)
    packed = packed.transpose(6, 0, 2, 4, 7, 1, 3, 5, 8).reshape(3, -1, HEADS, WT * WH * WW, head_dim)
    scores = jnp.einsum('nhqe,nhke->nhqk', packed[0].astype(jnp.float32), packed[1].astype(jnp.float32)) * head_dim ** (-0.5)
    weights = jax.nn.softmax(scores, axis=-1).astype(jnp.bfloat16)
    mixed_heads = jnp.einsum('nhqk,nhke->nhqe', weights.astype(jnp.float32), packed[2].astype(jnp.float32)).astype(jnp.bfloat16)
    mixed_heads = mixed_heads.reshape(frame_count // WT, row_count // WH, column_count // WW, HEADS, WT, WH, WW, head_dim)
    mixed_heads = mixed_heads.transpose(0, 4, 1, 5, 2, 6, 3, 7).reshape(-1, model_width)
    result_rows = jnp.dot(mixed_heads, w_out, preferred_element_type=jnp.float32)
    return result_rows.reshape(frame_count, row_count, column_count, model_width)

def pixel_gradient(stream_rows, pixel_rows, masked, w_head):
    row_total, pixel_count = pixel_rows.shape
    group_size = pixel_count // 3
    raw_pixels = pixel_rows.astype(jnp.float32).reshape(row_total, 3, group_size)
    center = raw_pixels - lax.optimization_barrier(jnp.mean(raw_pixels, axis=-1, keepdims=True))
    spread = jnp.sqrt(lax.optimization_barrier(jnp.sum(center * center, axis=-1, keepdims=True)) / (group_size - 1))
    target = (center / (spread + 1e-06)).reshape(row_total, pixel_count)

    def pixel_loss(values):
        normed = layer_norm(values).astype(jnp.bfloat16)
        predicted = jnp.dot(normed, w_head, preferred_element_type=jnp.float32)
        errors = predicted - target
        return 0.5 * jnp.sum(masked[:, None] * errors * errors)
    return jax.grad(pixel_loss)(stream_rows)

def reference(visible, slot_pos, window_shift, mask_token, w_qkv, w_out, w_head, pixels):
    is_live = slot_pos >= 0
    local_pos = jnp.where(is_live, slot_pos, 0).astype(jnp.int32)
    slab_index = jnp.arange(N_TM, dtype=jnp.int32)[:, None, None, None]
    band_index = jnp.arange(N_ROW, dtype=jnp.int32)[None, None, :, None]
    frame_pos = slab_index * TL + local_pos // (HL * W)
    row_pos = band_index * HL + local_pos // W % HL
    global_pos = (frame_pos * NH + row_pos) * W + local_pos % W
    global_pos = jnp.where(is_live, global_pos, TOKENS).astype(jnp.int32).reshape(-1)
    live_flat = is_live.reshape(-1)
    visible_grid = jnp.zeros((TOKENS, D), jnp.float32).at[global_pos].set(visible.reshape(-1, D).astype(jnp.float32), mode='drop')
    seen_flags = jnp.zeros((TOKENS,), jnp.float32).at[global_pos].set(1.0, mode='drop')
    token_index = jnp.arange(TOKENS, dtype=jnp.int32)
    position_rows = position_table(token_index // (NH * W), token_index // W % NH, token_index % W, D)
    start_rows = jnp.where(seen_flags[:, None] > 0, visible_grid, mask_token.astype(jnp.float32)[None, :])
    embedded = (start_rows + position_rows).astype(jnp.bfloat16)
    stream = embedded.astype(jnp.float32).reshape(NT, NH, W, D)

    def attend(grid_block):
        results = []
        for group in range(W // WW):
            piece = grid_block[:, :, group * WW:(group + 1) * WW]
            time_offset = window_shift[0, group]
            row_offset = window_shift[1, group]
            rolled = jnp.roll(piece, (time_offset, row_offset), axis=(0, 1))
            results.append(jnp.roll(window_core(rolled, w_qkv, w_out), (-time_offset, -row_offset), axis=(0, 1)))
        return jnp.concatenate(results, axis=2)
    attn_full, pull_back = jax.vjp(attend, stream)
    attn_value = attn_full.astype(jnp.bfloat16)
    residual = stream + attn_value.astype(jnp.float32)
    masked = 1.0 - seen_flags
    grad_stream = pixel_gradient(residual.reshape(TOKENS, D), pixels.reshape(TOKENS, PIX), masked, w_head)
    grad_attn = lax.optimization_barrier(grad_stream.astype(jnp.bfloat16)).astype(jnp.float32)
    grad_core = pull_back(grad_attn.reshape(NT, NH, W, D))[0]
    grad_embedded = grad_stream + grad_core.reshape(TOKENS, D)
    picked = grad_embedded[jnp.minimum(global_pos, TOKENS - 1)] * live_flat[:, None].astype(jnp.float32)
    d_visible = picked.astype(jnp.bfloat16).reshape(visible.shape)
    d_mask_token = lax.optimization_barrier(jnp.sum(masked[:, None] * grad_embedded, axis=0)) * TOKENS ** (-0.5)
    return (d_visible, d_mask_token)
```

```python
import functools
import math

import jax
import jax.numpy as jnp
from jax import lax
from jax.experimental import pallas as pl
from jax.experimental.pallas import tpu as pltpu
from jax.sharding import PartitionSpec as P

HEADS = 16
WT = 2
WH = 4
WW = 8
EPS = 1e-05
TILE = 16
LANES = 128
MESH = pl.DeviceIdType.MESH
F32 = jnp.float32
BF16 = jnp.bfloat16


def sinusoid(coordinate, channel_count):
    half_count = channel_count // 2
    frequency = jnp.exp(-math.log(10000.0) * jnp.arange(half_count, dtype=F32) / half_count)
    angles = coordinate.astype(F32)[..., None] * frequency
    return jnp.concatenate([jnp.sin(angles), jnp.cos(angles)], axis=-1)


def nt_dot(a, b):
    return lax.dot_general(a, b, (((1,), (1,)), ((), ())), preferred_element_type=F32)


def tn_dot(a, b):
    return lax.dot_general(a, b, (((0,), (0,)), ((), ())), preferred_element_type=F32)


def nn_dot(a, b):
    return jnp.dot(a, b, preferred_element_type=F32)


def norm_parts(values):
    center = values - jnp.mean(values, axis=-1, keepdims=True)
    scale = lax.rsqrt(jnp.mean(center * center, axis=-1, keepdims=True) + EPS)
    return center * scale, scale


def norm_grad(cotangent, normed, scale):
    return scale * (
        cotangent
        - jnp.mean(cotangent, axis=-1, keepdims=True)
        - normed * jnp.mean(cotangent * normed, axis=-1, keepdims=True)
    )


def spread_kernel(slabs, bands, x_ref, out_ref, send_sem, recv_sem):
    i, d = lax.axis_index("tm"), lax.axis_index("row")
    after = lax.rem(i + 1, slabs)
    before = lax.rem(i + slabs - 1, slabs)
    barrier = pltpu.get_barrier_semaphore()
    for o in range(1, bands):
        pl.semaphore_signal(
            barrier, inc=1, device_id=(i, lax.rem(d + o, bands)), device_id_type=MESH
        )
    for o in range(bands):
        pl.semaphore_signal(
            barrier, inc=1, device_id=(before, lax.rem(d + o, bands)), device_id_type=MESH
        )
    pl.semaphore_wait(barrier, 2 * bands - 1)
    copies = []
    for q, slab in ((1, after), (0, i)):
        for o in range(1 - q, bands):
            e = lax.rem(d + o, bands)
            copy = pltpu.make_async_remote_copy(
                src_ref=x_ref.at[e],
                dst_ref=out_ref.at[q * bands + d],
                send_sem=send_sem.at[q * bands + o],
                recv_sem=recv_sem.at[q * bands + o],
                device_id=(slab, e),
                device_id_type=MESH,
            )
            copy.start()
            copies.append((q, o, copy))
    out_ref[d] = x_ref[d]
    for q, o, copy in copies:
        s = lax.rem(d + bands - o, bands)
        arriving = pltpu.make_async_remote_copy(
            src_ref=x_ref.at[0],
            dst_ref=out_ref.at[q * bands + s],
            send_sem=send_sem.at[q * bands + o],
            recv_sem=recv_sem.at[q * bands + o],
            device_id=(i, lax.rem(d + 1, bands)),
            device_id_type=MESH,
        )
        arriving.wait_recv()
        copy.wait_send()


def collect_kernel(
    slabs, bands, x_ref, sum_ref, out_ref, total_ref,
    got, row_sums, slab_sums, mine,
    send_sem, recv_sem, row_send, row_recv, slab_send, slab_recv,
):
    i, d = lax.axis_index("tm"), lax.axis_index("row")
    after = lax.rem(i + 1, slabs)
    before = lax.rem(i + slabs - 1, slabs)
    barrier = pltpu.get_barrier_semaphore()
    for o in range(1, bands):
        pl.semaphore_signal(
            barrier, inc=1, device_id=(i, lax.rem(d + o, bands)), device_id_type=MESH
        )
    for o in range(bands):
        pl.semaphore_signal(
            barrier, inc=1, device_id=(after, lax.rem(d + o, bands)), device_id_type=MESH
        )
    for o in range(1, slabs):
        pl.semaphore_signal(
            barrier, inc=1, device_id=(lax.rem(i + o, slabs), d), device_id_type=MESH
        )
    pl.semaphore_wait(barrier, 2 * bands - 1 + slabs - 1)

    sums = []
    for o in range(1, bands):
        copy = pltpu.make_async_remote_copy(
            src_ref=sum_ref,
            dst_ref=row_sums.at[d],
            send_sem=row_send.at[o],
            recv_sem=row_recv.at[o],
            device_id=(i, lax.rem(d + o, bands)),
            device_id_type=MESH,
        )
        copy.start()
        sums.append(copy)
    copies = []
    for q, slab in ((1, before), (0, i)):
        for o in range(1 - q, bands):
            s = lax.rem(d + o, bands)
            copy = pltpu.make_async_remote_copy(
                src_ref=x_ref.at[q * bands + s],
                dst_ref=got.at[q * bands + d],
                send_sem=send_sem.at[q * bands + o],
                recv_sem=recv_sem.at[q * bands + o],
                device_id=(slab, s),
                device_id_type=MESH,
            )
            copy.start()
            copies.append((q, o, copy))
    got[d] = x_ref[d]
    row_sums[d] = sum_ref[...]
    for o, copy in enumerate(sums, 1):
        s = lax.rem(d + bands - o, bands)
        pltpu.make_async_remote_copy(
            src_ref=sum_ref,
            dst_ref=row_sums.at[s],
            send_sem=row_send.at[o],
            recv_sem=row_recv.at[o],
            device_id=(i, lax.rem(d + 1, bands)),
            device_id_type=MESH,
        ).wait_recv()
        copy.wait_send()
    total = row_sums[0]
    for s in range(1, bands):
        total = total + row_sums[s]
    mine[...] = total
    slab_sums[i] = total
    sums = []
    for o in range(1, slabs):
        copy = pltpu.make_async_remote_copy(
            src_ref=mine,
            dst_ref=slab_sums.at[i],
            send_sem=slab_send.at[o],
            recv_sem=slab_recv.at[o],
            device_id=(lax.rem(i + o, slabs), d),
            device_id_type=MESH,
        )
        copy.start()
        sums.append(copy)
    for q, o, copy in copies:
        s = lax.rem(d + bands - o, bands)
        pltpu.make_async_remote_copy(
            src_ref=x_ref.at[0],
            dst_ref=got.at[q * bands + s],
            send_sem=send_sem.at[q * bands + o],
            recv_sem=recv_sem.at[q * bands + o],
            device_id=(i, lax.rem(d + 1, bands)),
            device_id_type=MESH,
        ).wait_recv()
        copy.wait_send()
    for e in range(bands):
        f = (e + 1) % bands
        value = got[e, 1].astype(F32) + got[f, 0].astype(F32)
        value = value + got[bands + e, 1].astype(F32) + got[bands + f, 0].astype(F32)
        out_ref[e] = value.astype(BF16)
    for o, copy in enumerate(sums, 1):
        s = lax.rem(i + slabs - o, slabs)
        pltpu.make_async_remote_copy(
            src_ref=mine,
            dst_ref=slab_sums.at[s],
            send_sem=slab_send.at[o],
            recv_sem=slab_recv.at[o],
            device_id=(lax.rem(i + 1, slabs), d),
            device_id_type=MESH,
        ).wait_recv()
        copy.wait_send()
    total = slab_sums[0]
    for s in range(1, slabs):
        total = total + slab_sums[s]
    total_ref[...] = total


def block_kernel(
    slots, grid,
    shift_ref, recv_ref, token_ref, mask_ref, pos_t_ref, pos_h_ref, pos_c_ref,
    w_qkv_ref, w_out_ref, w_head_ref, own_ref, rows_ref, frames_ref, corner_ref,
    picked_ref, sum_ref,
    joined, pix, probs, mixed, d_qkv,
):
    frames, rows, columns = grid
    groups = columns // WW
    tokens = frames * rows * columns
    width = mask_ref.shape[1]
    head_dim = width // HEADS
    parts = TILE // slots
    chunk = width // parts
    total_rows = recv_ref.shape[0]
    rim_t, rim_h = WT - 1, WH - 1

    index = recv_ref[:, chunk:].astype(F32)
    index = jnp.concatenate([index] * (tokens // LANES), axis=1)
    pieces = []
    for block in range(total_rows // TILE):
        q = block // (total_rows // TILE // 2)
        line = token_ref[2 * q + block % 2 : 2 * q + block % 2 + 1, :]
        pieces.append(jnp.broadcast_to(line, (TILE, tokens)))
    hit = (index == jnp.concatenate(pieces, axis=0)).astype(F32)
    part_of = lax.broadcasted_iota(jnp.int32, (total_rows, tokens), 0) // slots % parts
    part_of_t = lax.broadcasted_iota(jnp.int32, (tokens, total_rows), 1) // slots % parts
    hit_t = hit.T
    seen = jnp.max(hit_t, axis=1, keepdims=True)
    masked = 1.0 - seen
    packed_rows = recv_ref[:, :chunk]
    start = jnp.concatenate(
        [
            nn_dot(jnp.where(part_of_t == j, hit_t, 0.0).astype(BF16), packed_rows)
            for j in range(parts)
        ],
        axis=1,
    )
    start = jnp.where(seen > 0, start, mask_ref[...].astype(F32))

    order = [
        (fw, hw, g, ft, r)
        for fw in range(frames // WT)
        for hw in range(rows // WH)
        for g in range(groups)
        for ft in range(WT)
        for r in range(WH)
    ]
    pieces = []
    for fw, hw, g, ft, r in order:
        t_line = g * frames + fw * WT + ft
        h_line = g * rows + hw * WH + r
        pieces.append(
            jnp.concatenate(
                [
                    jnp.broadcast_to(pos_t_ref[t_line : t_line + 1], (WW, pos_t_ref.shape[1])),
                    jnp.broadcast_to(pos_h_ref[h_line : h_line + 1], (WW, pos_h_ref.shape[1])),
                    pos_c_ref[g * WW : (g + 1) * WW],
                ],
                axis=1,
            )
        )
    embedded = (start + jnp.concatenate(pieces, axis=0)).astype(BF16).astype(F32)

    normed, scale = norm_parts(embedded)
    qkv = nn_dot(normed.astype(BF16), w_qkv_ref[...]).astype(BF16)

    window = WT * WH * WW
    span = 2 * window
    pair = 2 * head_dim
    same = (
        lax.broadcasted_iota(jnp.int32, (span, span), 0) // window
        == lax.broadcasted_iota(jnp.int32, (span, span), 1) // window
    )
    lane = lax.broadcasted_iota(jnp.int32, (span, pair), 1) // head_dim
    zero = jnp.zeros((span, pair), BF16)

    def block_of(values, b, at):
        return values[b * span : (b + 1) * span, at : at + pair]

    for b in range(tokens // span):
        for p in range(HEADS // 2):
            q = block_of(qkv, b, p * pair)
            k = block_of(qkv, b, width + p * pair)
            v = block_of(qkv, b, 2 * width + p * pair)
            out = None
            for h in range(2):
                scores = nt_dot(q, jnp.where(lane == h, k, zero)) * head_dim ** (-0.5)
                scores = jnp.where(same, scores, -jnp.inf)
                weights = jnp.exp(scores - jnp.max(scores, axis=-1, keepdims=True))
                weights = weights / jnp.sum(weights, axis=-1, keepdims=True)
                probs[(b * HEADS // 2 + p) * 2 + h] = weights
                part = nn_dot(weights.astype(BF16), jnp.where(lane == h, v, zero))
                out = part if out is None else out + part
            mixed[b * span : (b + 1) * span, p * pair : (p + 1) * pair] = out.astype(BF16)
    attn = nn_dot(mixed[...], w_out_ref[...]).astype(BF16)
    residual = embedded + attn.astype(F32)

    for t in range(frames):
        for h in range(rows):
            joined[(t + rim_t) * (rows + rim_h) + h + rim_h] = own_ref[t, h]
        for h in range(rim_h):
            joined[(t + rim_t) * (rows + rim_h) + h] = rows_ref[t, h]
    for t in range(rim_t):
        for h in range(rows):
            joined[t * (rows + rim_h) + h + rim_h] = frames_ref[t, h]
        for h in range(rim_h):
            joined[t * (rows + rim_h) + h] = corner_ref[t, h]
    for n, (fw, hw, g, ft, r) in enumerate(order):
        t = fw * WT + ft + rim_t - shift_ref[0, g]
        h = hw * WH + r + rim_h - shift_ref[1, g]
        pix[n * WW : (n + 1) * WW, :] = joined[t * (rows + rim_h) + h][
            g * WW : (g + 1) * WW, :
        ].astype(F32)
    group_size = pix.shape[1] // 3
    targets = []
    for c in range(3):
        raw = pix[:, c * group_size : (c + 1) * group_size]
        center = raw - jnp.mean(raw, axis=-1, keepdims=True)
        spread = jnp.sqrt(jnp.sum(center * center, axis=-1, keepdims=True) / (group_size - 1))
        targets.append(center / (spread + 1e-06))
    target = jnp.concatenate(targets, axis=1)

    normed_out, scale_out = norm_parts(residual)
    predicted = nn_dot(normed_out.astype(BF16), w_head_ref[...])
    errors = (predicted - target) * masked
    d_normed_out = nt_dot(errors.astype(BF16), w_head_ref[...]).astype(BF16).astype(F32)
    grad_residual = norm_grad(d_normed_out, normed_out, scale_out)
    d_mixed = nt_dot(grad_residual.astype(BF16), w_out_ref[...]).astype(BF16)

    for b in range(tokens // span):
        for p in range(HEADS // 2):
            q = block_of(qkv, b, p * pair)
            k = block_of(qkv, b, width + p * pair)
            v = block_of(qkv, b, 2 * width + p * pair)
            d_out = block_of(d_mixed, b, p * pair)
            dq = dk = dv = None
            for h in range(2):
                mine = lane == h
                weights = probs[(b * HEADS // 2 + p) * 2 + h]
                d_weights = nt_dot(d_out, jnp.where(mine, v, zero)).astype(BF16).astype(F32)
                inner = jnp.sum(weights * d_weights, axis=-1, keepdims=True)
                d_scores = weights * (d_weights - inner) * head_dim ** (-0.5)
                d_scores = d_scores.astype(BF16)
                terms = (
                    nn_dot(d_scores, jnp.where(mine, k, zero)),
                    tn_dot(d_scores, jnp.where(mine, q, zero)),
                    tn_dot(weights.astype(BF16), jnp.where(mine, d_out, zero)),
                )
                if h == 0:
                    dq, dk, dv = terms
                else:
                    dq, dk, dv = dq + terms[0], dk + terms[1], dv + terms[2]
            for m, value in enumerate((dq, dk, dv)):
                at = m * width + p * pair
                d_qkv[b * span : (b + 1) * span, at : at + pair] = value.astype(BF16)
    d_normed = nt_dot(d_qkv[...], w_qkv_ref[...]).astype(BF16).astype(F32)
    grad = grad_residual + norm_grad(d_normed, normed, scale)

    line = jnp.sum(grad * masked, axis=0, keepdims=True)
    for j in range(width // LANES):
        sum_ref[j : j + 1, :] = line[:, j * LANES : (j + 1) * LANES]
    rounded = grad.astype(BF16)
    picked = None
    for j in range(parts):
        term = nn_dot(
            jnp.where(part_of == j, hit, 0.0).astype(BF16), rounded[:, j * chunk : (j + 1) * chunk]
        )
        picked = term if picked is None else picked + term
    picked_ref[...] = picked.astype(BF16)


def per_device(visible, slot_pos, window_shift, mask_token, w_qkv, w_out, w_head, pixels):
    frames, rows, columns, pixel_count = pixels.shape
    width = mask_token.shape[0]
    tokens = frames * rows * columns
    bands, slots = slot_pos.shape[2:]
    slabs = lax.axis_size("tm")
    groups = columns // WW
    parts = TILE // slots
    chunk = width // parts
    rim_t, rim_h = WT - 1, WH - 1
    i, d = lax.axis_index("tm"), lax.axis_index("row")
    vmem = pl.BlockSpec(memory_space=pltpu.VMEM)

    both = ("tm", "row")
    slab_ring = [(a, (a + 1) % slabs) for a in range(slabs)]
    band_ring = [(a, (a + 1) % bands) for a in range(bands)]
    corner_ring = [
        (a * bands + b, (a + 1) % slabs * bands + (b + 1) % bands)
        for a in range(slabs)
        for b in range(bands)
    ]
    row_halo = lax.ppermute(pixels[:, rows - rim_h :], "row", band_ring)
    frame_halo = lax.ppermute(pixels[frames - rim_t :], "tm", slab_ring)
    corner_halo = lax.ppermute(pixels[frames - rim_t :, rows - rim_h :], both, corner_ring)

    packed = visible.reshape(bands, slots, parts, chunk).transpose(0, 2, 1, 3)
    packed = packed.reshape(bands, TILE, chunk)
    index = jnp.broadcast_to(
        slot_pos.reshape(bands, 1, slots, 1), (bands, parts, slots, LANES)
    ).reshape(bands, TILE, LANES)
    packed = jnp.concatenate([packed, index.astype(BF16)], axis=-1)
    packed = jnp.stack([jnp.roll(packed, 1, axis=0), packed], axis=1)
    wide = chunk + LANES
    received = pl.pallas_call(
        functools.partial(spread_kernel, slabs, bands),
        out_shape=jax.ShapeDtypeStruct((2 * bands, 2, TILE, wide), BF16),
        in_specs=[vmem],
        out_specs=vmem,
        scratch_shapes=[
            pltpu.SemaphoreType.DMA((2 * bands,)),
            pltpu.SemaphoreType.DMA((2 * bands,)),
        ],
        compiler_params=pltpu.CompilerParams(collective_id=0, has_side_effects=True),
        name="spread",
    )(packed)

    n = jnp.arange(tokens, dtype=jnp.int32)
    column = n % WW
    r = n // WW % WH
    ft = n // (WW * WH) % WT
    g = n // (WW * WH * WT) % groups
    hw = n // (WW * WH * WT * groups) % (rows // WH)
    fw = n // (WW * WH * WT * groups * (rows // WH))
    t_shift = sum(jnp.where(g == a, window_shift[0, a], 0) for a in range(groups))
    h_shift = sum(jnp.where(g == a, window_shift[1, a], 0) for a in range(groups))
    t = fw * WT + ft - t_shift
    h = hw * WH + r - h_shift
    local = (t % frames * rows + h % rows) * columns + g * WW + column
    token_index = jnp.stack(
        [
            jnp.where(((t < 0) == (q == 1)) & ((h < 0) == (k == 0)), local, -2)
            for q in range(2)
            for k in range(2)
        ]
    ).astype(F32)
    quarter = width // 4
    rest = (width - quarter) // 2
    t_all = (i * frames + jnp.arange(frames) - window_shift[0][:, None]) % (frames * slabs)
    h_all = (d * rows + jnp.arange(rows) - window_shift[1][:, None]) % (rows * bands)
    pos_t = sinusoid(t_all.reshape(-1), quarter)
    pos_h = sinusoid(h_all.reshape(-1), rest)
    pos_c = sinusoid(jnp.arange(columns), width - quarter - rest)

    total_rows = 2 * bands * 2 * TILE
    flops = 4 * tokens * width * (w_qkv.shape[1] + width + pixel_count)
    picked, partial_sum = pl.pallas_call(
        functools.partial(block_kernel, slots, (frames, rows, columns)),
        out_shape=(
            jax.ShapeDtypeStruct((total_rows, chunk), BF16),
            jax.ShapeDtypeStruct((width // LANES, LANES), F32),
        ),
        in_specs=[pl.BlockSpec(memory_space=pltpu.SMEM)] + [vmem] * 13,
        out_specs=(vmem, vmem),
        scratch_shapes=[
            pltpu.VMEM(((frames + rim_t) * (rows + rim_h), columns, pixel_count), BF16),
            pltpu.VMEM((tokens, pixel_count), F32),
            pltpu.VMEM(
                (HEADS * tokens // (2 * WT * WH * WW), 2 * WT * WH * WW, 2 * WT * WH * WW), F32
            ),
            pltpu.VMEM((tokens, width), BF16),
            pltpu.VMEM((tokens, 3 * width), BF16),
        ],
        compiler_params=pltpu.CompilerParams(vmem_limit_bytes=56 * 2**20),
        cost_estimate=pl.CostEstimate(
            flops=flops, bytes_accessed=16 * 2**20, transcendentals=HEADS * tokens * 128
        ),
        name="block",
    )(
        window_shift, received.reshape(total_rows, wide), token_index, mask_token[None, :],
        pos_t, pos_h, pos_c, w_qkv, w_out, w_head, pixels, row_halo, frame_halo, corner_halo,
    )

    lines = width // LANES
    returned, total = pl.pallas_call(
        functools.partial(collect_kernel, slabs, bands),
        out_shape=(
            jax.ShapeDtypeStruct((bands, TILE, chunk), BF16),
            jax.ShapeDtypeStruct((lines, LANES), F32),
        ),
        in_specs=[vmem, vmem],
        out_specs=(vmem, vmem),
        scratch_shapes=[
            pltpu.VMEM((2 * bands, 2, TILE, chunk), BF16),
            pltpu.VMEM((bands, lines, LANES), F32),
            pltpu.VMEM((slabs, lines, LANES), F32),
            pltpu.VMEM((lines, LANES), F32),
            pltpu.SemaphoreType.DMA((2 * bands,)),
            pltpu.SemaphoreType.DMA((2 * bands,)),
            pltpu.SemaphoreType.DMA((bands,)),
            pltpu.SemaphoreType.DMA((bands,)),
            pltpu.SemaphoreType.DMA((slabs,)),
            pltpu.SemaphoreType.DMA((slabs,)),
        ],
        compiler_params=pltpu.CompilerParams(collective_id=1, has_side_effects=True),
        name="collect",
    )(picked.reshape(2 * bands, 2, TILE, chunk), partial_sum)
    d_visible = returned.reshape(bands, parts, slots, chunk).transpose(0, 2, 1, 3)
    grad_scale = (tokens * slabs * bands) ** (-0.5)
    return d_visible.reshape(visible.shape), total.reshape(width) * grad_scale


def solution(mesh):
    placed = (
        P("tm", "row", None, None, None),
        P("tm", "row", None, None),
        P(),
        P(),
        P(),
        P(),
        P(),
        P("tm", "row", None, None),
    )
    return jax.shard_map(
        per_device,
        mesh=mesh,
        in_specs=placed,
        out_specs=(P("tm", "row", None, None, None), P()),
        check_vma=False,
    )
```

```python
import functools
import math

import jax
import jax.numpy as jnp
from jax import lax
from jax.experimental import pallas as pl
from jax.experimental.pallas import tpu as pltpu
from jax.sharding import PartitionSpec as P

HEADS = 16
WT = 2
WH = 4
WW = 8
EPS = 1e-05
TILE = 16
LANES = 128
MESH = pl.DeviceIdType.MESH
F32 = jnp.float32
BF16 = jnp.bfloat16


def sinusoid(coordinates, channel_count):
    half_count = channel_count // 2
    lane = lax.broadcasted_iota(jnp.int32, (1, channel_count), 1)
    late = lane >= half_count
    step = jnp.where(late, lane - half_count, lane).astype(F32)
    angles = coordinates * jnp.exp(-math.log(10000.0) * step / half_count)
    return jnp.where(late, jnp.cos(angles), jnp.sin(angles))


def nt_dot(a, b):
    return lax.dot_general(a, b, (((1,), (1,)), ((), ())), preferred_element_type=F32)


def tn_dot(a, b):
    return lax.dot_general(a, b, (((0,), (0,)), ((), ())), preferred_element_type=F32)


def nn_dot(a, b):
    return jnp.dot(a, b, preferred_element_type=F32)


def norm_parts(values):
    center = values - jnp.mean(values, axis=-1, keepdims=True)
    scale = lax.rsqrt(jnp.mean(center * center, axis=-1, keepdims=True) + EPS)
    return center * scale, scale


def norm_grad(cotangent, normed, scale):
    return scale * (
        cotangent
        - jnp.mean(cotangent, axis=-1, keepdims=True)
        - normed * jnp.mean(cotangent * normed, axis=-1, keepdims=True)
    )


def spread_kernel(
    slabs, bands, slot_ref, visible_ref, pixel_ref,
    out_ref, row_ref, frame_ref, corner_ref,
    x_ref, send_sem, recv_sem, halo_send, halo_recv,
):
    i, d = lax.axis_index("tm"), lax.axis_index("row")
    after = lax.rem(i + 1, slabs)
    before = lax.rem(i + slabs - 1, slabs)
    barrier = pltpu.get_barrier_semaphore()
    for o in range(1, bands):
        pl.semaphore_signal(
            barrier, inc=1, device_id=(i, lax.rem(d + o, bands)), device_id_type=MESH
        )
    for o in range(bands):
        pl.semaphore_signal(
            barrier, inc=1, device_id=(before, lax.rem(d + o, bands)), device_id_type=MESH
        )
    pl.semaphore_wait(barrier, 2 * bands - 1)
    frames, rows = pixel_ref.shape[:2]
    rim_t, rim_h = WT - 1, WH - 1
    next_band = lax.rem(d + 1, bands)
    last_rows = pl.ds(rows - rim_h, rim_h)
    last_frames = pl.ds(frames - rim_t, rim_t)
    halos = []
    for m, (source, target, device) in enumerate(
        (
            (pixel_ref.at[:, last_rows], row_ref, (i, next_band)),
            (pixel_ref.at[last_frames], frame_ref, (after, d)),
            (pixel_ref.at[last_frames, last_rows], corner_ref, (after, next_band)),
        )
    ):
        copy = pltpu.make_async_remote_copy(
            src_ref=source,
            dst_ref=target,
            send_sem=halo_send.at[m],
            recv_sem=halo_recv.at[m],
            device_id=device,
            device_id_type=MESH,
        )
        copy.start()
        halos.append(copy)
    slots, width = visible_ref.shape[1:]
    parts = TILE // slots
    chunk = width // parts
    slot_of = lax.broadcasted_iota(jnp.int32, (TILE, LANES), 0) % slots
    for e in range(bands):
        values = visible_ref[e].astype(F32)
        values = jnp.concatenate(
            [values[:, j * chunk : (j + 1) * chunk] for j in range(parts)], axis=0
        ).astype(BF16)
        index = jnp.full((TILE, LANES), slot_ref[e, 0], jnp.int32)
        for c in range(1, slots):
            index = jnp.where(slot_of == c, slot_ref[e, c], index)
        index = index.astype(F32).astype(BF16)
        for at, k in ((e, 1), ((e + 1) % bands, 0)):
            x_ref[at, k, :, :chunk] = values
            x_ref[at, k, :, chunk:] = index
    copies = []
    for q, slab in ((1, after), (0, i)):
        for o in range(1 - q, bands):
            e = lax.rem(d + o, bands)
            copy = pltpu.make_async_remote_copy(
                src_ref=x_ref.at[e],
                dst_ref=out_ref.at[q * bands + d],
                send_sem=send_sem.at[q * bands + o],
                recv_sem=recv_sem.at[q * bands + o],
                device_id=(slab, e),
                device_id_type=MESH,
            )
            copy.start()
            copies.append((q, o, copy))
    out_ref[d] = x_ref[d]
    for q, o, copy in copies:
        s = lax.rem(d + bands - o, bands)
        arriving = pltpu.make_async_remote_copy(
            src_ref=x_ref.at[0],
            dst_ref=out_ref.at[q * bands + s],
            send_sem=send_sem.at[q * bands + o],
            recv_sem=recv_sem.at[q * bands + o],
            device_id=(i, lax.rem(d + 1, bands)),
            device_id_type=MESH,
        )
        arriving.wait_recv()
        copy.wait_send()
    for copy in halos:
        copy.wait()


def collect_kernel(
    slabs, bands, grad_scale, x_ref, sum_ref, out_ref, total_ref,
    got, row_sums, slab_sums, mine,
    send_sem, recv_sem, row_send, row_recv, slab_send, slab_recv,
):
    i, d = lax.axis_index("tm"), lax.axis_index("row")
    after = lax.rem(i + 1, slabs)
    before = lax.rem(i + slabs - 1, slabs)
    barrier = pltpu.get_barrier_semaphore()
    for o in range(1, bands):
        pl.semaphore_signal(
            barrier, inc=1, device_id=(i, lax.rem(d + o, bands)), device_id_type=MESH
        )
    for o in range(bands):
        pl.semaphore_signal(
            barrier, inc=1, device_id=(after, lax.rem(d + o, bands)), device_id_type=MESH
        )
    for o in range(1, slabs):
        pl.semaphore_signal(
            barrier, inc=1, device_id=(lax.rem(i + o, slabs), d), device_id_type=MESH
        )
    pl.semaphore_wait(barrier, 2 * bands - 1 + slabs - 1)

    sums = []
    for o in range(1, bands):
        copy = pltpu.make_async_remote_copy(
            src_ref=sum_ref,
            dst_ref=row_sums.at[d],
            send_sem=row_send.at[o],
            recv_sem=row_recv.at[o],
            device_id=(i, lax.rem(d + o, bands)),
            device_id_type=MESH,
        )
        copy.start()
        sums.append(copy)
    copies = []
    for q, slab in ((1, before), (0, i)):
        for o in range(1 - q, bands):
            s = lax.rem(d + o, bands)
            copy = pltpu.make_async_remote_copy(
                src_ref=x_ref.at[q * bands + s],
                dst_ref=got.at[q * bands + d],
                send_sem=send_sem.at[q * bands + o],
                recv_sem=recv_sem.at[q * bands + o],
                device_id=(slab, s),
                device_id_type=MESH,
            )
            copy.start()
            copies.append((q, o, copy))
    got[d] = x_ref[d]
    row_sums[d] = sum_ref[...]
    for o, copy in enumerate(sums, 1):
        s = lax.rem(d + bands - o, bands)
        pltpu.make_async_remote_copy(
            src_ref=sum_ref,
            dst_ref=row_sums.at[s],
            send_sem=row_send.at[o],
            recv_sem=row_recv.at[o],
            device_id=(i, lax.rem(d + 1, bands)),
            device_id_type=MESH,
        ).wait_recv()
        copy.wait_send()
    total = row_sums[0]
    for s in range(1, bands):
        total = total + row_sums[s]
    mine[...] = total
    slab_sums[i] = total
    sums = []
    for o in range(1, slabs):
        copy = pltpu.make_async_remote_copy(
            src_ref=mine,
            dst_ref=slab_sums.at[i],
            send_sem=slab_send.at[o],
            recv_sem=slab_recv.at[o],
            device_id=(lax.rem(i + o, slabs), d),
            device_id_type=MESH,
        )
        copy.start()
        sums.append(copy)
    for q, o, copy in copies:
        s = lax.rem(d + bands - o, bands)
        pltpu.make_async_remote_copy(
            src_ref=x_ref.at[0],
            dst_ref=got.at[q * bands + s],
            send_sem=send_sem.at[q * bands + o],
            recv_sem=recv_sem.at[q * bands + o],
            device_id=(i, lax.rem(d + 1, bands)),
            device_id_type=MESH,
        ).wait_recv()
        copy.wait_send()
    for e in range(bands):
        f = (e + 1) % bands
        value = got[e, 1].astype(F32) + got[f, 0].astype(F32)
        value = value + got[bands + e, 1].astype(F32) + got[bands + f, 0].astype(F32)
        slots = out_ref.shape[1]
        value = jnp.concatenate(
            [value[j * slots : (j + 1) * slots] for j in range(TILE // slots)], axis=1
        )
        out_ref[e] = value.astype(BF16)
    for o, copy in enumerate(sums, 1):
        s = lax.rem(i + slabs - o, slabs)
        pltpu.make_async_remote_copy(
            src_ref=mine,
            dst_ref=slab_sums.at[s],
            send_sem=slab_send.at[o],
            recv_sem=slab_recv.at[o],
            device_id=(lax.rem(i + 1, slabs), d),
            device_id_type=MESH,
        ).wait_recv()
        copy.wait_send()
    total = slab_sums[0]
    for s in range(1, slabs):
        total = total + slab_sums[s]
    total = total * grad_scale
    for j in range(total.shape[0]):
        total_ref[:, j * LANES : (j + 1) * LANES] = total[j : j + 1]


def block_kernel(
    slots, grid, slabs, bands,
    shift_ref, recv_ref, mask_ref,
    w_qkv_hbm, w_out_hbm, w_head_hbm, own_ref, rows_ref, frames_ref, corner_ref,
    picked_ref, sum_ref,
    joined, pix, probs, mixed, d_qkv, w_qkv_ref, w_out_ref, w_head_ref, sems,
):
    frames, rows, columns = grid
    groups = columns // WW
    tokens = frames * rows * columns
    width = mask_ref.shape[1]
    head_dim = width // HEADS
    parts = TILE // slots
    chunk = width // parts
    total_rows = recv_ref.shape[0]
    rim_t, rim_h = WT - 1, WH - 1

    inner_rows, outer_rows = pl.ds(rim_h, rows), pl.ds(0, rim_h)
    inner_frames, outer_frames = pl.ds(rim_t, frames), pl.ds(0, rim_t)
    loads = [
        pltpu.make_async_copy(source, target, sems.at[m])
        for m, (source, target) in enumerate(
            (
                (w_qkv_hbm, w_qkv_ref),
                (w_out_hbm, w_out_ref),
                (own_ref, joined.at[inner_frames, inner_rows]),
                (rows_ref, joined.at[inner_frames, outer_rows]),
                (frames_ref, joined.at[outer_frames, inner_rows]),
                (corner_ref, joined.at[outer_frames, outer_rows]),
                (w_head_hbm, w_head_ref),
            )
        )
    ]
    for load in loads:
        load.start()

    n = lax.broadcasted_iota(jnp.int32, (1, tokens), 1)
    group = n // (WW * WH * WT) % groups
    t_shift = h_shift = jnp.zeros((1, tokens), jnp.int32)
    for a in range(groups):
        t_shift = jnp.where(group == a, shift_ref[0, a], t_shift)
        h_shift = jnp.where(group == a, shift_ref[1, a], h_shift)
    per_pair = WW * WH * WT * groups
    t = n // (per_pair * (rows // WH)) * WT + n // (WW * WH) % WT - t_shift
    h = n // per_pair % (rows // WH) * WH + n // WW % WH - h_shift
    local = jnp.where(t < 0, t + frames, t) * rows + jnp.where(h < 0, h + rows, h)
    local = local * columns + group * WW + n % WW
    lines = [
        jnp.where(((t < 0) == (q == 1)) & ((h < 0) == (k == 0)), local, -2).astype(F32)
        for q in range(2)
        for k in range(2)
    ]
    quarter = width // 4
    rest = (width - quarter) // 2
    i, d = lax.axis_index("tm"), lax.axis_index("row")
    t_count, h_count = frames * slabs, rows * bands

    def table(count, total, base, shifts, channels):
        row = lax.broadcasted_iota(jnp.int32, (groups * count, channels), 0)
        at = base + row % count + total
        for a in range(groups):
            at = jnp.where(row // count == a, at - shift_ref[shifts, a], at)
        at = jnp.where(at >= total, at - total, at)
        return sinusoid(at.astype(F32), channels)

    pos_t = table(frames, t_count, i * frames, 0, quarter)
    pos_h = table(rows, h_count, d * rows, 1, rest)
    last = width - quarter - rest
    pos_c = sinusoid(lax.broadcasted_iota(jnp.int32, (columns, last), 0).astype(F32), last)

    index = recv_ref[:, chunk:].astype(F32)
    index = jnp.concatenate([index] * (tokens // LANES), axis=1)
    pieces = []
    for block in range(total_rows // TILE):
        q = block // (total_rows // TILE // 2)
        line = lines[2 * q + block % 2]
        pieces.append(jnp.broadcast_to(line, (TILE, tokens)))
    hit = (index == jnp.concatenate(pieces, axis=0)).astype(F32)
    part_of = lax.broadcasted_iota(jnp.int32, (total_rows, tokens), 0) // slots % parts
    part_of_t = lax.broadcasted_iota(jnp.int32, (tokens, total_rows), 1) // slots % parts
    hit_t = hit.T
    seen = jnp.max(hit_t, axis=1, keepdims=True)
    masked = 1.0 - seen
    packed_rows = recv_ref[:, :chunk]
    start = jnp.concatenate(
        [
            nn_dot(jnp.where(part_of_t == j, hit_t, 0.0).astype(BF16), packed_rows)
            for j in range(parts)
        ],
        axis=1,
    )
    start = jnp.where(seen > 0, start, mask_ref[...].astype(F32))

    order = [
        (fw, hw, g, ft, r)
        for fw in range(frames // WT)
        for hw in range(rows // WH)
        for g in range(groups)
        for ft in range(WT)
        for r in range(WH)
    ]
    pieces = []
    for fw, hw, g, ft, r in order:
        t_line = g * frames + fw * WT + ft
        h_line = g * rows + hw * WH + r
        pieces.append(
            jnp.concatenate(
                [
                    jnp.broadcast_to(pos_t[t_line : t_line + 1], (WW, quarter)),
                    jnp.broadcast_to(pos_h[h_line : h_line + 1], (WW, rest)),
                    pos_c[g * WW : (g + 1) * WW],
                ],
                axis=1,
            )
        )
    embedded = (start + jnp.concatenate(pieces, axis=0)).astype(BF16).astype(F32)

    normed, scale = norm_parts(embedded)
    loads[0].wait()
    qkv = nn_dot(normed.astype(BF16), w_qkv_ref[...]).astype(BF16)

    window = WT * WH * WW
    span = 2 * window
    pair = 2 * head_dim
    same = (
        lax.broadcasted_iota(jnp.int32, (span, span), 0) // window
        == lax.broadcasted_iota(jnp.int32, (span, span), 1) // window
    )
    lane = lax.broadcasted_iota(jnp.int32, (span, pair), 1) // head_dim
    zero = jnp.zeros((span, pair), BF16)

    def halves(values):
        return jnp.concatenate(
            [jnp.where(lane == 0, values, zero), jnp.where(lane == 1, values, zero)], axis=0
        )

    def block_of(values, b, at):
        return values[b * span : (b + 1) * span, at : at + pair]

    for b in range(tokens // span):
        for p in range(HEADS // 2):
            q = block_of(qkv, b, p * pair)
            k = block_of(qkv, b, width + p * pair)
            v = block_of(qkv, b, 2 * width + p * pair)
            scores = nt_dot(q, halves(k)) * head_dim ** (-0.5)
            both = []
            for m in range(2):
                part = jnp.where(same, scores[:, m * span : (m + 1) * span], -jnp.inf)
                weights = jnp.exp(part - jnp.max(part, axis=-1, keepdims=True))
                both.append(weights * (1.0 / jnp.sum(weights, axis=-1, keepdims=True)))
            weights = jnp.concatenate(both, axis=1)
            probs[b * HEADS // 2 + p] = weights
            out = nn_dot(weights.astype(BF16), halves(v))
            mixed[b * span : (b + 1) * span, p * pair : (p + 1) * pair] = out.astype(BF16)
    loads[1].wait()
    attn = nn_dot(mixed[...], w_out_ref[...]).astype(BF16)
    residual = embedded + attn.astype(F32)

    for load in loads[2:6]:
        load.wait()
    for n, (fw, hw, g, ft, r) in enumerate(order):
        t = fw * WT + ft + rim_t - shift_ref[0, g]
        h = hw * WH + r + rim_h - shift_ref[1, g]
        pix[n * WW : (n + 1) * WW, :] = joined[t, h][
            g * WW : (g + 1) * WW, :
        ].astype(F32)
    group_size = pix.shape[1] // 3
    targets = []
    for c in range(3):
        raw = pix[:, c * group_size : (c + 1) * group_size]
        center = raw - jnp.mean(raw, axis=-1, keepdims=True)
        spread = jnp.sqrt(jnp.sum(center * center, axis=-1, keepdims=True) / (group_size - 1))
        targets.append(center * (1.0 / (spread + 1e-06)))
    target = jnp.concatenate(targets, axis=1)

    normed_out, scale_out = norm_parts(residual)
    loads[6].wait()
    predicted = nn_dot(normed_out.astype(BF16), w_head_ref[...])
    errors = (predicted - target) * masked
    d_normed_out = nt_dot(errors.astype(BF16), w_head_ref[...]).astype(BF16).astype(F32)
    grad_residual = norm_grad(d_normed_out, normed_out, scale_out)
    d_mixed = nt_dot(grad_residual.astype(BF16), w_out_ref[...]).astype(BF16)

    for b in range(tokens // span):
        for p in range(HEADS // 2):
            q = block_of(qkv, b, p * pair)
            k = block_of(qkv, b, width + p * pair)
            v = block_of(qkv, b, 2 * width + p * pair)
            d_out = block_of(d_mixed, b, p * pair)
            weights = probs[b * HEADS // 2 + p]
            d_weights = nt_dot(d_out, halves(v)).astype(BF16).astype(F32)
            both = []
            for m in range(2):
                w = weights[:, m * span : (m + 1) * span]
                dw = d_weights[:, m * span : (m + 1) * span]
                inner = jnp.sum(w * dw, axis=-1, keepdims=True)
                both.append(w * (dw - inner) * head_dim ** (-0.5))
            d_scores = jnp.concatenate(both, axis=1).astype(BF16)
            dq = nn_dot(d_scores, halves(k))
            dk = tn_dot(d_scores, q)
            dv = tn_dot(weights.astype(BF16), d_out)
            dk = jnp.where(lane == 0, dk[:span], dk[span:])
            dv = jnp.where(lane == 0, dv[:span], dv[span:])
            for m, value in enumerate((dq, dk, dv)):
                at = m * width + p * pair
                d_qkv[b * span : (b + 1) * span, at : at + pair] = value.astype(BF16)
    d_normed = nt_dot(d_qkv[...], w_qkv_ref[...]).astype(BF16).astype(F32)
    grad = grad_residual + norm_grad(d_normed, normed, scale)

    line = jnp.sum(grad * masked, axis=0, keepdims=True)
    for j in range(width // LANES):
        sum_ref[j : j + 1, :] = line[:, j * LANES : (j + 1) * LANES]
    rounded = grad.astype(BF16)
    picked = None
    for j in range(parts):
        term = nn_dot(
            jnp.where(part_of == j, hit, 0.0).astype(BF16), rounded[:, j * chunk : (j + 1) * chunk]
        )
        picked = term if picked is None else picked + term
    picked_ref[...] = picked.astype(BF16)


def per_device(visible, slot_pos, window_shift, mask_token, w_qkv, w_out, w_head, pixels):
    frames, rows, columns, pixel_count = pixels.shape
    width = mask_token.shape[0]
    tokens = frames * rows * columns
    bands, slots = slot_pos.shape[2:]
    slabs = lax.axis_size("tm")
    parts = TILE // slots
    chunk = width // parts
    rim_t, rim_h = WT - 1, WH - 1
    vmem = pl.BlockSpec(memory_space=pltpu.VMEM)
    smem = pl.BlockSpec(memory_space=pltpu.SMEM)
    anywhere = pl.BlockSpec(memory_space=pl.ANY)
    wide = chunk + LANES
    received, row_halo, frame_halo, corner_halo = pl.pallas_call(
        functools.partial(spread_kernel, slabs, bands),
        out_shape=(
            jax.ShapeDtypeStruct((2 * bands, 2, TILE, wide), BF16),
            jax.ShapeDtypeStruct((frames, rim_h, columns, pixel_count), BF16),
            jax.ShapeDtypeStruct((rim_t, rows, columns, pixel_count), BF16),
            jax.ShapeDtypeStruct((rim_t, rim_h, columns, pixel_count), BF16),
        ),
        in_specs=[smem, vmem, anywhere],
        out_specs=(vmem, anywhere, anywhere, anywhere),
        scratch_shapes=[
            pltpu.VMEM((bands, 2, TILE, wide), BF16),
            pltpu.SemaphoreType.DMA((2 * bands,)),
            pltpu.SemaphoreType.DMA((2 * bands,)),
            pltpu.SemaphoreType.DMA((3,)),
            pltpu.SemaphoreType.DMA((3,)),
        ],
        compiler_params=pltpu.CompilerParams(collective_id=0, has_side_effects=True),
        name="spread",
    )(slot_pos.reshape(bands, slots), visible.reshape(bands, slots, width), pixels)

    total_rows = 2 * bands * 2 * TILE
    flops = 4 * tokens * width * (w_qkv.shape[1] + width + pixel_count)
    picked, partial_sum = pl.pallas_call(
        functools.partial(block_kernel, slots, (frames, rows, columns), slabs, bands),
        out_shape=(
            jax.ShapeDtypeStruct((total_rows, chunk), BF16),
            jax.ShapeDtypeStruct((width // LANES, LANES), F32),
        ),
        in_specs=[smem, vmem, vmem] + [anywhere] * 7,
        out_specs=(vmem, vmem),
        scratch_shapes=[
            pltpu.VMEM((frames + rim_t, rows + rim_h, columns, pixel_count), BF16),
            pltpu.VMEM((tokens, pixel_count), F32),
            pltpu.VMEM(
                (HEADS * tokens // (4 * WT * WH * WW), 2 * WT * WH * WW, 4 * WT * WH * WW), F32
            ),
            pltpu.VMEM((tokens, width), BF16),
            pltpu.VMEM((tokens, 3 * width), BF16),
            pltpu.VMEM(w_qkv.shape, BF16),
            pltpu.VMEM(w_out.shape, BF16),
            pltpu.VMEM(w_head.shape, BF16),
            pltpu.SemaphoreType.DMA((7,)),
        ],
        compiler_params=pltpu.CompilerParams(vmem_limit_bytes=56 * 2**20),
        cost_estimate=pl.CostEstimate(
            flops=flops, bytes_accessed=16 * 2**20, transcendentals=HEADS * tokens * 128
        ),
        name="block",
    )(
        window_shift, received.reshape(total_rows, wide), mask_token[None, :],
        w_qkv, w_out, w_head, pixels, row_halo, frame_halo, corner_halo,
    )

    lines = width // LANES
    returned, total = pl.pallas_call(
        functools.partial(collect_kernel, slabs, bands, (tokens * slabs * bands) ** (-0.5)),
        out_shape=(
            jax.ShapeDtypeStruct((bands, slots, width), BF16),
            jax.ShapeDtypeStruct((1, width), F32),
        ),
        in_specs=[vmem, vmem],
        out_specs=(vmem, vmem),
        scratch_shapes=[
            pltpu.VMEM((2 * bands, 2, TILE, chunk), BF16),
            pltpu.VMEM((bands, lines, LANES), F32),
            pltpu.VMEM((slabs, lines, LANES), F32),
            pltpu.VMEM((lines, LANES), F32),
            pltpu.SemaphoreType.DMA((2 * bands,)),
            pltpu.SemaphoreType.DMA((2 * bands,)),
            pltpu.SemaphoreType.DMA((bands,)),
            pltpu.SemaphoreType.DMA((bands,)),
            pltpu.SemaphoreType.DMA((slabs,)),
            pltpu.SemaphoreType.DMA((slabs,)),
        ],
        compiler_params=pltpu.CompilerParams(collective_id=1, has_side_effects=True),
        name="collect",
    )(picked.reshape(2 * bands, 2, TILE, chunk), partial_sum)
    return returned.reshape(visible.shape), total.reshape(width)


def solution(mesh):
    placed = (
        P("tm", "row", None, None, None),
        P("tm", "row", None, None),
        P(),
        P(),
        P(),
        P(),
        P(),
        P("tm", "row", None, None),
    )
    return jax.shard_map(
        per_device,
        mesh=mesh,
        in_specs=placed,
        out_specs=(P("tm", "row", None, None, None), P()),
        check_vma=False,
    )
```

```python
import functools
import math

import jax
import jax.numpy as jnp
from jax import lax
from jax.experimental import pallas as pl
from jax.experimental.pallas import tpu as pltpu
from jax.sharding import PartitionSpec as P

HEADS = 16
WT = 2
WH = 4
WW = 8
EPS = 1e-05
TILE = 16
LANES = 128
MESH = pl.DeviceIdType.MESH
F32 = jnp.float32
BF16 = jnp.bfloat16


def sinusoid(coordinates, channel_count):
    half_count = channel_count // 2
    lane = lax.broadcasted_iota(jnp.int32, (1, channel_count), 1)
    late = lane >= half_count
    step = jnp.where(late, lane - half_count, lane).astype(F32)
    angles = coordinates * jnp.exp(-math.log(10000.0) * step / half_count)
    return jnp.where(late, jnp.cos(angles), jnp.sin(angles))


def nt_dot(a, b):
    return lax.dot_general(a, b, (((1,), (1,)), ((), ())), preferred_element_type=F32)


def tn_dot(a, b):
    return lax.dot_general(a, b, (((0,), (0,)), ((), ())), preferred_element_type=F32)


def nn_dot(a, b):
    return jnp.dot(a, b, preferred_element_type=F32)


def norm_parts(values):
    center = values - jnp.mean(values, axis=-1, keepdims=True)
    scale = lax.rsqrt(jnp.mean(center * center, axis=-1, keepdims=True) + EPS)
    return center * scale, scale


def norm_grad(cotangent, normed, scale):
    return scale * (
        cotangent
        - jnp.mean(cotangent, axis=-1, keepdims=True)
        - normed * jnp.mean(cotangent * normed, axis=-1, keepdims=True)
    )


def exchange(
    slabs, bands, slot_ref, visible_ref, pixel_ref, out_ref, joined,
    x_ref, send_sem, recv_sem, halo_send, halo_recv,
):
    i, d = lax.axis_index("tm"), lax.axis_index("row")
    after = lax.rem(i + 1, slabs)
    before = lax.rem(i + slabs - 1, slabs)
    barrier = pltpu.get_barrier_semaphore()
    for o in range(1, bands):
        pl.semaphore_signal(
            barrier, inc=1, device_id=(i, lax.rem(d + o, bands)), device_id_type=MESH
        )
    for o in range(bands):
        pl.semaphore_signal(
            barrier, inc=1, device_id=(before, lax.rem(d + o, bands)), device_id_type=MESH
        )
    pl.semaphore_wait(barrier, 2 * bands - 1)
    frames, rows = pixel_ref.shape[:2]
    rim_t, rim_h = WT - 1, WH - 1
    next_band = lax.rem(d + 1, bands)
    last_rows = pl.ds(rows - rim_h, rim_h)
    last_frames = pl.ds(frames - rim_t, rim_t)
    inner_rows, outer_rows = pl.ds(rim_h, rows), pl.ds(0, rim_h)
    inner_frames, outer_frames = pl.ds(rim_t, frames), pl.ds(0, rim_t)
    halos = []
    for m, (source, target, device) in enumerate(
        (
            (pixel_ref.at[:, last_rows], joined.at[inner_frames, outer_rows], (i, next_band)),
            (pixel_ref.at[last_frames], joined.at[outer_frames, inner_rows], (after, d)),
            (
                pixel_ref.at[last_frames, last_rows],
                joined.at[outer_frames, outer_rows],
                (after, next_band),
            ),
        )
    ):
        copy = pltpu.make_async_remote_copy(
            src_ref=source,
            dst_ref=target,
            send_sem=halo_send.at[m],
            recv_sem=halo_recv.at[m],
            device_id=device,
            device_id_type=MESH,
        )
        copy.start()
        halos.append(copy)
    slots, width = visible_ref.shape[3:]
    parts = TILE // slots
    chunk = width // parts
    slot_of = lax.broadcasted_iota(jnp.int32, (TILE, LANES), 0) % slots
    for e in range(bands):
        values = visible_ref[0, 0, e].astype(F32)
        values = jnp.concatenate(
            [values[:, j * chunk : (j + 1) * chunk] for j in range(parts)], axis=0
        ).astype(BF16)
        index = jnp.full((TILE, LANES), slot_ref[0, 0, e, 0], jnp.int32)
        for c in range(1, slots):
            index = jnp.where(slot_of == c, slot_ref[0, 0, e, c], index)
        index = index.astype(F32).astype(BF16)
        for at, k in ((e, 1), ((e + 1) % bands, 0)):
            x_ref[at, k, :, :chunk] = values
            x_ref[at, k, :, chunk:] = index
    copies = []
    for q, slab in ((1, after), (0, i)):
        for o in range(1 - q, bands):
            e = lax.rem(d + o, bands)
            copy = pltpu.make_async_remote_copy(
                src_ref=x_ref.at[e],
                dst_ref=out_ref.at[q * bands + d],
                send_sem=send_sem.at[q * bands + o],
                recv_sem=recv_sem.at[q * bands + o],
                device_id=(slab, e),
                device_id_type=MESH,
            )
            copy.start()
            copies.append((q, o, copy))
    out_ref[d] = x_ref[d]
    for q, o, copy in copies:
        s = lax.rem(d + bands - o, bands)
        arriving = pltpu.make_async_remote_copy(
            src_ref=x_ref.at[0],
            dst_ref=out_ref.at[q * bands + s],
            send_sem=send_sem.at[q * bands + o],
            recv_sem=recv_sem.at[q * bands + o],
            device_id=(i, lax.rem(d + 1, bands)),
            device_id_type=MESH,
        )
        arriving.wait_recv()
        copy.wait_send()
    return halos


def collect_kernel(
    slabs, bands, grad_scale, x_ref, sum_ref, out_ref, total_ref,
    got, row_sums, slab_sums, mine,
    send_sem, recv_sem, row_send, row_recv, slab_send, slab_recv,
):
    i, d = lax.axis_index("tm"), lax.axis_index("row")
    after = lax.rem(i + 1, slabs)
    before = lax.rem(i + slabs - 1, slabs)
    barrier = pltpu.get_barrier_semaphore()
    for o in range(1, bands):
        pl.semaphore_signal(
            barrier, inc=1, device_id=(i, lax.rem(d + o, bands)), device_id_type=MESH
        )
    for o in range(bands):
        pl.semaphore_signal(
            barrier, inc=1, device_id=(after, lax.rem(d + o, bands)), device_id_type=MESH
        )
    for o in range(1, slabs):
        pl.semaphore_signal(
            barrier, inc=1, device_id=(lax.rem(i + o, slabs), d), device_id_type=MESH
        )
    pl.semaphore_wait(barrier, 2 * bands - 1 + slabs - 1)

    sums = []
    for o in range(1, bands):
        copy = pltpu.make_async_remote_copy(
            src_ref=sum_ref,
            dst_ref=row_sums.at[d],
            send_sem=row_send.at[o],
            recv_sem=row_recv.at[o],
            device_id=(i, lax.rem(d + o, bands)),
            device_id_type=MESH,
        )
        copy.start()
        sums.append(copy)
    copies = []
    for q, slab in ((1, before), (0, i)):
        for o in range(1 - q, bands):
            s = lax.rem(d + o, bands)
            copy = pltpu.make_async_remote_copy(
                src_ref=x_ref.at[q * bands + s],
                dst_ref=got.at[q * bands + d],
                send_sem=send_sem.at[q * bands + o],
                recv_sem=recv_sem.at[q * bands + o],
                device_id=(slab, s),
                device_id_type=MESH,
            )
            copy.start()
            copies.append((q, o, copy))
    got[d] = x_ref[d]
    row_sums[d] = sum_ref[...]
    for o, copy in enumerate(sums, 1):
        s = lax.rem(d + bands - o, bands)
        pltpu.make_async_remote_copy(
            src_ref=sum_ref,
            dst_ref=row_sums.at[s],
            send_sem=row_send.at[o],
            recv_sem=row_recv.at[o],
            device_id=(i, lax.rem(d + 1, bands)),
            device_id_type=MESH,
        ).wait_recv()
        copy.wait_send()
    total = row_sums[0]
    for s in range(1, bands):
        total = total + row_sums[s]
    mine[...] = total
    slab_sums[i] = total
    sums = []
    for o in range(1, slabs):
        copy = pltpu.make_async_remote_copy(
            src_ref=mine,
            dst_ref=slab_sums.at[i],
            send_sem=slab_send.at[o],
            recv_sem=slab_recv.at[o],
            device_id=(lax.rem(i + o, slabs), d),
            device_id_type=MESH,
        )
        copy.start()
        sums.append(copy)
    for q, o, copy in copies:
        s = lax.rem(d + bands - o, bands)
        pltpu.make_async_remote_copy(
            src_ref=x_ref.at[0],
            dst_ref=got.at[q * bands + s],
            send_sem=send_sem.at[q * bands + o],
            recv_sem=recv_sem.at[q * bands + o],
            device_id=(i, lax.rem(d + 1, bands)),
            device_id_type=MESH,
        ).wait_recv()
        copy.wait_send()
    for e in range(bands):
        f = (e + 1) % bands
        value = got[e, 1].astype(F32) + got[f, 0].astype(F32)
        value = value + got[bands + e, 1].astype(F32) + got[bands + f, 0].astype(F32)
        slots = out_ref.shape[1]
        value = jnp.concatenate(
            [value[j * slots : (j + 1) * slots] for j in range(TILE // slots)], axis=1
        )
        out_ref[e] = value.astype(BF16)
    for o, copy in enumerate(sums, 1):
        s = lax.rem(i + slabs - o, slabs)
        pltpu.make_async_remote_copy(
            src_ref=mine,
            dst_ref=slab_sums.at[s],
            send_sem=slab_send.at[o],
            recv_sem=slab_recv.at[o],
            device_id=(lax.rem(i + 1, slabs), d),
            device_id_type=MESH,
        ).wait_recv()
        copy.wait_send()
    total = slab_sums[0]
    for s in range(1, slabs):
        total = total + slab_sums[s]
    total = total * grad_scale
    for j in range(total.shape[0]):
        total_ref[:, j * LANES : (j + 1) * LANES] = total[j : j + 1]


def block_kernel(
    slots, grid, slabs, bands,
    slot_ref, shift_ref, visible_ref, mask_ref,
    w_qkv_hbm, w_out_hbm, w_head_hbm, own_ref,
    picked_ref, sum_ref,
    joined, pix, probs, mixed, d_qkv, w_qkv_ref, w_out_ref, w_head_ref, sems,
    got_ref, x_ref, send_sem, recv_sem, halo_send, halo_recv,
):
    frames, rows, columns = grid
    groups = columns // WW
    tokens = frames * rows * columns
    width = mask_ref.shape[0]
    head_dim = width // HEADS
    parts = TILE // slots
    chunk = width // parts
    total_rows = 2 * bands * 2 * TILE
    rim_t, rim_h = WT - 1, WH - 1

    loads = [
        pltpu.make_async_copy(source, target, sems.at[m])
        for m, (source, target) in enumerate(
            (
                (w_qkv_hbm, w_qkv_ref),
                (w_out_hbm, w_out_ref),
                (own_ref, joined.at[pl.ds(rim_t, frames), pl.ds(rim_h, rows)]),
                (w_head_hbm, w_head_ref),
            )
        )
    ]
    for load in loads:
        load.start()
    halos = exchange(
        slabs, bands, slot_ref, visible_ref, own_ref, got_ref, joined,
        x_ref, send_sem, recv_sem, halo_send, halo_recv,
    )

    n = lax.broadcasted_iota(jnp.int32, (1, tokens), 1)
    group = n // (WW * WH * WT) % groups
    t_shift = h_shift = jnp.zeros((1, tokens), jnp.int32)
    for a in range(groups):
        t_shift = jnp.where(group == a, shift_ref[0, a], t_shift)
        h_shift = jnp.where(group == a, shift_ref[1, a], h_shift)
    per_pair = WW * WH * WT * groups
    t = n // (per_pair * (rows // WH)) * WT + n // (WW * WH) % WT - t_shift
    h = n // per_pair % (rows // WH) * WH + n // WW % WH - h_shift
    local = jnp.where(t < 0, t + frames, t) * rows + jnp.where(h < 0, h + rows, h)
    local = local * columns + group * WW + n % WW
    lines = [
        jnp.where(((t < 0) == (q == 1)) & ((h < 0) == (k == 0)), local, -2).astype(F32)
        for q in range(2)
        for k in range(2)
    ]
    quarter = width // 4
    rest = (width - quarter) // 2
    i, d = lax.axis_index("tm"), lax.axis_index("row")
    t_count, h_count = frames * slabs, rows * bands

    def table(count, total, base, shifts, channels):
        row = lax.broadcasted_iota(jnp.int32, (groups * count, channels), 0)
        at = base + row % count + total
        for a in range(groups):
            at = jnp.where(row // count == a, at - shift_ref[shifts, a], at)
        at = jnp.where(at >= total, at - total, at)
        return sinusoid(at.astype(F32), channels)

    pos_t = table(frames, t_count, i * frames, 0, quarter)
    pos_h = table(rows, h_count, d * rows, 1, rest)
    last = width - quarter - rest
    pos_c = sinusoid(lax.broadcasted_iota(jnp.int32, (columns, last), 0).astype(F32), last)

    received = got_ref[...].reshape(total_rows, chunk + LANES)
    index = received[:, chunk:].astype(F32)
    index = jnp.concatenate([index] * (tokens // LANES), axis=1)
    pieces = []
    for block in range(total_rows // TILE):
        q = block // (total_rows // TILE // 2)
        line = lines[2 * q + block % 2]
        pieces.append(jnp.broadcast_to(line, (TILE, tokens)))
    hit = (index == jnp.concatenate(pieces, axis=0)).astype(F32)
    part_of = lax.broadcasted_iota(jnp.int32, (total_rows, tokens), 0) // slots % parts
    part_of_t = lax.broadcasted_iota(jnp.int32, (tokens, total_rows), 1) // slots % parts
    hit_t = hit.T
    seen = jnp.max(hit_t, axis=1, keepdims=True)
    masked = 1.0 - seen
    packed_rows = received[:, :chunk]
    start = jnp.concatenate(
        [
            nn_dot(jnp.where(part_of_t == j, hit_t, 0.0).astype(BF16), packed_rows)
            for j in range(parts)
        ],
        axis=1,
    )
    start = jnp.where(seen > 0, start, mask_ref[...].astype(F32)[None, :])

    order = [
        (fw, hw, g, ft, r)
        for fw in range(frames // WT)
        for hw in range(rows // WH)
        for g in range(groups)
        for ft in range(WT)
        for r in range(WH)
    ]
    pieces = []
    for fw, hw, g, ft, r in order:
        t_line = g * frames + fw * WT + ft
        h_line = g * rows + hw * WH + r
        pieces.append(
            jnp.concatenate(
                [
                    jnp.broadcast_to(pos_t[t_line : t_line + 1], (WW, quarter)),
                    jnp.broadcast_to(pos_h[h_line : h_line + 1], (WW, rest)),
                    pos_c[g * WW : (g + 1) * WW],
                ],
                axis=1,
            )
        )
    embedded = (start + jnp.concatenate(pieces, axis=0)).astype(BF16).astype(F32)

    normed, scale = norm_parts(embedded)
    loads[0].wait()
    qkv = nn_dot(normed.astype(BF16), w_qkv_ref[...]).astype(BF16)

    window = WT * WH * WW
    span = 2 * window
    pair = 2 * head_dim
    same = (
        lax.broadcasted_iota(jnp.int32, (span, span), 0) // window
        == lax.broadcasted_iota(jnp.int32, (span, span), 1) // window
    )
    lane = lax.broadcasted_iota(jnp.int32, (span, pair), 1) // head_dim
    zero = jnp.zeros((span, pair), BF16)

    def halves(values):
        return jnp.concatenate(
            [jnp.where(lane == 0, values, zero), jnp.where(lane == 1, values, zero)], axis=0
        )

    def block_of(values, b, at):
        return values[b * span : (b + 1) * span, at : at + pair]

    for b in range(tokens // span):
        for p in range(HEADS // 2):
            q = block_of(qkv, b, p * pair)
            k = block_of(qkv, b, width + p * pair)
            v = block_of(qkv, b, 2 * width + p * pair)
            scores = nt_dot(q, halves(k)) * head_dim ** (-0.5)
            both = []
            for m in range(2):
                part = jnp.where(same, scores[:, m * span : (m + 1) * span], -jnp.inf)
                weights = jnp.exp(part - jnp.max(part, axis=-1, keepdims=True))
                both.append(weights * (1.0 / jnp.sum(weights, axis=-1, keepdims=True)))
            weights = jnp.concatenate(both, axis=1)
            probs[b * HEADS // 2 + p] = weights
            out = nn_dot(weights.astype(BF16), halves(v))
            mixed[b * span : (b + 1) * span, p * pair : (p + 1) * pair] = out.astype(BF16)
    loads[1].wait()
    attn = nn_dot(mixed[...], w_out_ref[...]).astype(BF16)
    residual = embedded + attn.astype(F32)

    loads[2].wait()
    for copy in halos:
        copy.wait()
    for n, (fw, hw, g, ft, r) in enumerate(order):
        t = fw * WT + ft + rim_t - shift_ref[0, g]
        h = hw * WH + r + rim_h - shift_ref[1, g]
        pix[n * WW : (n + 1) * WW, :] = joined[t, h][
            g * WW : (g + 1) * WW, :
        ].astype(F32)
    group_size = pix.shape[1] // 3
    targets = []
    for c in range(3):
        raw = pix[:, c * group_size : (c + 1) * group_size]
        center = raw - jnp.mean(raw, axis=-1, keepdims=True)
        spread = jnp.sqrt(jnp.sum(center * center, axis=-1, keepdims=True) / (group_size - 1))
        targets.append(center * (1.0 / (spread + 1e-06)))
    target = jnp.concatenate(targets, axis=1)

    normed_out, scale_out = norm_parts(residual)
    loads[3].wait()
    predicted = nn_dot(normed_out.astype(BF16), w_head_ref[...])
    errors = (predicted - target) * masked
    d_normed_out = nt_dot(errors.astype(BF16), w_head_ref[...]).astype(BF16).astype(F32)
    grad_residual = norm_grad(d_normed_out, normed_out, scale_out)
    d_mixed = nt_dot(grad_residual.astype(BF16), w_out_ref[...]).astype(BF16)

    for b in range(tokens // span):
        for p in range(HEADS // 2):
            q = block_of(qkv, b, p * pair)
            k = block_of(qkv, b, width + p * pair)
            v = block_of(qkv, b, 2 * width + p * pair)
            d_out = block_of(d_mixed, b, p * pair)
            weights = probs[b * HEADS // 2 + p]
            d_weights = nt_dot(d_out, halves(v)).astype(BF16).astype(F32)
            both = []
            for m in range(2):
                w = weights[:, m * span : (m + 1) * span]
                dw = d_weights[:, m * span : (m + 1) * span]
                inner = jnp.sum(w * dw, axis=-1, keepdims=True)
                both.append(w * (dw - inner) * head_dim ** (-0.5))
            d_scores = jnp.concatenate(both, axis=1).astype(BF16)
            dq = nn_dot(d_scores, halves(k))
            dk = tn_dot(d_scores, q)
            dv = tn_dot(weights.astype(BF16), d_out)
            dk = jnp.where(lane == 0, dk[:span], dk[span:])
            dv = jnp.where(lane == 0, dv[:span], dv[span:])
            for m, value in enumerate((dq, dk, dv)):
                at = m * width + p * pair
                d_qkv[b * span : (b + 1) * span, at : at + pair] = value.astype(BF16)
    d_normed = nt_dot(d_qkv[...], w_qkv_ref[...]).astype(BF16).astype(F32)
    grad = grad_residual + norm_grad(d_normed, normed, scale)

    line = jnp.sum(grad * masked, axis=0, keepdims=True)
    for j in range(width // LANES):
        sum_ref[j : j + 1, :] = line[:, j * LANES : (j + 1) * LANES]
    rounded = grad.astype(BF16)
    picked = None
    for j in range(parts):
        term = nn_dot(
            jnp.where(part_of == j, hit, 0.0).astype(BF16), rounded[:, j * chunk : (j + 1) * chunk]
        )
        picked = term if picked is None else picked + term
    picked_ref[...] = picked.astype(BF16)


def per_device(visible, slot_pos, window_shift, mask_token, w_qkv, w_out, w_head, pixels):
    frames, rows, columns, pixel_count = pixels.shape
    width = mask_token.shape[0]
    tokens = frames * rows * columns
    bands, slots = slot_pos.shape[2:]
    slabs = lax.axis_size("tm")
    parts = TILE // slots
    chunk = width // parts
    rim_t, rim_h = WT - 1, WH - 1
    vmem = pl.BlockSpec(memory_space=pltpu.VMEM)
    smem = pl.BlockSpec(memory_space=pltpu.SMEM)
    anywhere = pl.BlockSpec(memory_space=pl.ANY)
    wide = chunk + LANES
    total_rows = 2 * bands * 2 * TILE
    flops = 4 * tokens * width * (w_qkv.shape[1] + width + pixel_count)
    picked, partial_sum = pl.pallas_call(
        functools.partial(block_kernel, slots, (frames, rows, columns), slabs, bands),
        out_shape=(
            jax.ShapeDtypeStruct((total_rows, chunk), BF16),
            jax.ShapeDtypeStruct((width // LANES, LANES), F32),
        ),
        in_specs=[smem, smem, vmem, vmem] + [anywhere] * 4,
        out_specs=(vmem, vmem),
        scratch_shapes=[
            pltpu.VMEM((frames + rim_t, rows + rim_h, columns, pixel_count), BF16),
            pltpu.VMEM((tokens, pixel_count), F32),
            pltpu.VMEM(
                (HEADS * tokens // (4 * WT * WH * WW), 2 * WT * WH * WW, 4 * WT * WH * WW), F32
            ),
            pltpu.VMEM((tokens, width), BF16),
            pltpu.VMEM((tokens, 3 * width), BF16),
            pltpu.VMEM(w_qkv.shape, BF16),
            pltpu.VMEM(w_out.shape, BF16),
            pltpu.VMEM(w_head.shape, BF16),
            pltpu.SemaphoreType.DMA((4,)),
            pltpu.VMEM((2 * bands, 2, TILE, wide), BF16),
            pltpu.VMEM((bands, 2, TILE, wide), BF16),
            pltpu.SemaphoreType.DMA((2 * bands,)),
            pltpu.SemaphoreType.DMA((2 * bands,)),
            pltpu.SemaphoreType.DMA((3,)),
            pltpu.SemaphoreType.DMA((3,)),
        ],
        compiler_params=pltpu.CompilerParams(
            collective_id=0, has_side_effects=True, vmem_limit_bytes=56 * 2**20
        ),
        cost_estimate=pl.CostEstimate(
            flops=flops, bytes_accessed=16 * 2**20, transcendentals=HEADS * tokens * 128
        ),
        name="block",
    )(
        slot_pos, window_shift, visible, mask_token, w_qkv, w_out, w_head, pixels,
    )

    lines = width // LANES
    returned, total = pl.pallas_call(
        functools.partial(collect_kernel, slabs, bands, (tokens * slabs * bands) ** (-0.5)),
        out_shape=(
            jax.ShapeDtypeStruct((bands, slots, width), BF16),
            jax.ShapeDtypeStruct((1, width), F32),
        ),
        in_specs=[vmem, vmem],
        out_specs=(vmem, vmem),
        scratch_shapes=[
            pltpu.VMEM((2 * bands, 2, TILE, chunk), BF16),
            pltpu.VMEM((bands, lines, LANES), F32),
            pltpu.VMEM((slabs, lines, LANES), F32),
            pltpu.VMEM((lines, LANES), F32),
            pltpu.SemaphoreType.DMA((2 * bands,)),
            pltpu.SemaphoreType.DMA((2 * bands,)),
            pltpu.SemaphoreType.DMA((bands,)),
            pltpu.SemaphoreType.DMA((bands,)),
            pltpu.SemaphoreType.DMA((slabs,)),
            pltpu.SemaphoreType.DMA((slabs,)),
        ],
        compiler_params=pltpu.CompilerParams(collective_id=1, has_side_effects=True),
        name="collect",
    )(picked.reshape(2 * bands, 2, TILE, chunk), partial_sum)
    return returned.reshape(visible.shape), total.reshape(width)


def solution(mesh):
    placed = (
        P("tm", "row", None, None, None),
        P("tm", "row", None, None),
        P(),
        P(),
        P(),
        P(),
        P(),
        P("tm", "row", None, None),
    )
    return jax.shard_map(
        per_device,
        mesh=mesh,
        in_specs=placed,
        out_specs=(P("tm", "row", None, None, None), P()),
        check_vma=False,
    )
```

```python
import functools
import math

import jax
import jax.numpy as jnp
from jax import lax
from jax.experimental import pallas as pl
from jax.experimental.pallas import tpu as pltpu
from jax.sharding import PartitionSpec as P

HEADS = 16
WT = 2
WH = 4
WW = 8
EPS = 1e-05
TILE = 16
LANES = 128
MESH = pl.DeviceIdType.MESH
F32 = jnp.float32
BF16 = jnp.bfloat16


def sinusoid(coordinates, channel_count):
    half_count = channel_count // 2
    lane = lax.broadcasted_iota(jnp.int32, (1, channel_count), 1)
    late = lane >= half_count
    step = jnp.where(late, lane - half_count, lane).astype(F32)
    angles = coordinates * jnp.exp(-math.log(10000.0) * step / half_count)
    return jnp.where(late, jnp.cos(angles), jnp.sin(angles))


def nt_dot(a, b):
    return lax.dot_general(a, b, (((1,), (1,)), ((), ())), preferred_element_type=F32)


def tn_dot(a, b):
    return lax.dot_general(a, b, (((0,), (0,)), ((), ())), preferred_element_type=F32)


def nn_dot(a, b):
    return jnp.dot(a, b, preferred_element_type=F32)


def norm_parts(values):
    center = values - jnp.mean(values, axis=-1, keepdims=True)
    scale = lax.rsqrt(jnp.mean(center * center, axis=-1, keepdims=True) + EPS)
    return center * scale, scale


def norm_grad(cotangent, normed, scale):
    return scale * (
        cotangent
        - jnp.mean(cotangent, axis=-1, keepdims=True)
        - normed * jnp.mean(cotangent * normed, axis=-1, keepdims=True)
    )


def exchange(
    slabs, bands, slot_ref, visible_ref, pixel_ref, out_ref, joined,
    x_ref, send_sem, recv_sem, halo_send, halo_recv,
):
    i, d = lax.axis_index("tm"), lax.axis_index("row")
    after = lax.rem(i + 1, slabs)
    before = lax.rem(i + slabs - 1, slabs)
    barrier = pltpu.get_barrier_semaphore()
    for o in range(1, bands):
        pl.semaphore_signal(
            barrier, inc=1, device_id=(i, lax.rem(d + o, bands)), device_id_type=MESH
        )
    for o in range(bands):
        pl.semaphore_signal(
            barrier, inc=1, device_id=(before, lax.rem(d + o, bands)), device_id_type=MESH
        )
    pl.semaphore_wait(barrier, 2 * bands - 1)
    frames, rows = pixel_ref.shape[:2]
    rim_t, rim_h = WT - 1, WH - 1
    next_band = lax.rem(d + 1, bands)
    last_rows = pl.ds(rows - rim_h, rim_h)
    last_frames = pl.ds(frames - rim_t, rim_t)
    slots, width = visible_ref.shape[3:]
    parts = TILE // slots
    chunk = width // parts
    slot_of = lax.broadcasted_iota(jnp.int32, (TILE, LANES), 0) % slots
    for e in range(bands):
        values = visible_ref[0, 0, e].astype(F32)
        values = jnp.concatenate(
            [values[:, j * chunk : (j + 1) * chunk] for j in range(parts)], axis=0
        ).astype(BF16)
        index = jnp.full((TILE, LANES), slot_ref[0, 0, e, 0], jnp.int32)
        for c in range(1, slots):
            index = jnp.where(slot_of == c, slot_ref[0, 0, e, c], index)
        index = index.astype(F32).astype(BF16)
        for at, k in ((e, 1), ((e + 1) % bands, 0)):
            x_ref[at, k, :, :chunk] = values
            x_ref[at, k, :, chunk:] = index
    copies = []
    for q, slab in ((1, after), (0, i)):
        for o in range(1 - q, bands):
            e = lax.rem(d + o, bands)
            copy = pltpu.make_async_remote_copy(
                src_ref=x_ref.at[e],
                dst_ref=out_ref.at[q * bands + d],
                send_sem=send_sem.at[q * bands + o],
                recv_sem=recv_sem.at[q * bands + o],
                device_id=(slab, e),
                device_id_type=MESH,
            )
            copy.start()
            copies.append((q, o, copy))
    inner_rows, outer_rows = pl.ds(rim_h, rows), pl.ds(0, rim_h)
    inner_frames, outer_frames = pl.ds(rim_t, frames), pl.ds(0, rim_t)
    halos = []
    for m, (source, target, device) in enumerate(
        (
            (pixel_ref.at[:, last_rows], joined.at[inner_frames, outer_rows], (i, next_band)),
            (pixel_ref.at[last_frames], joined.at[outer_frames, inner_rows], (after, d)),
            (
                pixel_ref.at[last_frames, last_rows],
                joined.at[outer_frames, outer_rows],
                (after, next_band),
            ),
        )
    ):
        copy = pltpu.make_async_remote_copy(
            src_ref=source,
            dst_ref=target,
            send_sem=halo_send.at[m],
            recv_sem=halo_recv.at[m],
            device_id=device,
            device_id_type=MESH,
        )
        copy.start()
        halos.append(copy)
    out_ref[d] = x_ref[d]
    for q, o, copy in copies:
        s = lax.rem(d + bands - o, bands)
        arriving = pltpu.make_async_remote_copy(
            src_ref=x_ref.at[0],
            dst_ref=out_ref.at[q * bands + s],
            send_sem=send_sem.at[q * bands + o],
            recv_sem=recv_sem.at[q * bands + o],
            device_id=(i, lax.rem(d + 1, bands)),
            device_id_type=MESH,
        )
        arriving.wait_recv()
        copy.wait_send()
    return halos


def collect_kernel(
    slabs, bands, grad_scale, x_ref, sum_ref, out_ref, total_ref,
    got, row_sums, slab_sums, mine,
    send_sem, recv_sem, row_send, row_recv, slab_send, slab_recv,
):
    i, d = lax.axis_index("tm"), lax.axis_index("row")
    after = lax.rem(i + 1, slabs)
    before = lax.rem(i + slabs - 1, slabs)
    barrier = pltpu.get_barrier_semaphore()
    for o in range(1, bands):
        pl.semaphore_signal(
            barrier, inc=1, device_id=(i, lax.rem(d + o, bands)), device_id_type=MESH
        )
    for o in range(bands):
        pl.semaphore_signal(
            barrier, inc=1, device_id=(after, lax.rem(d + o, bands)), device_id_type=MESH
        )
    for o in range(1, slabs):
        pl.semaphore_signal(
            barrier, inc=1, device_id=(lax.rem(i + o, slabs), d), device_id_type=MESH
        )
    pl.semaphore_wait(barrier, 2 * bands - 1 + slabs - 1)

    sums = []
    for o in range(1, bands):
        copy = pltpu.make_async_remote_copy(
            src_ref=sum_ref,
            dst_ref=row_sums.at[d],
            send_sem=row_send.at[o],
            recv_sem=row_recv.at[o],
            device_id=(i, lax.rem(d + o, bands)),
            device_id_type=MESH,
        )
        copy.start()
        sums.append(copy)
    copies = []
    for q, slab in ((1, before), (0, i)):
        for o in range(1 - q, bands):
            s = lax.rem(d + o, bands)
            copy = pltpu.make_async_remote_copy(
                src_ref=x_ref.at[q * bands + s],
                dst_ref=got.at[q * bands + d],
                send_sem=send_sem.at[q * bands + o],
                recv_sem=recv_sem.at[q * bands + o],
                device_id=(slab, s),
                device_id_type=MESH,
            )
            copy.start()
            copies.append((q, o, copy))
    got[d] = x_ref[d]
    row_sums[d] = sum_ref[...]
    for o, copy in enumerate(sums, 1):
        s = lax.rem(d + bands - o, bands)
        pltpu.make_async_remote_copy(
            src_ref=sum_ref,
            dst_ref=row_sums.at[s],
            send_sem=row_send.at[o],
            recv_sem=row_recv.at[o],
            device_id=(i, lax.rem(d + 1, bands)),
            device_id_type=MESH,
        ).wait_recv()
        copy.wait_send()
    total = row_sums[0]
    for s in range(1, bands):
        total = total + row_sums[s]
    mine[...] = total
    slab_sums[i] = total
    sums = []
    for o in range(1, slabs):
        copy = pltpu.make_async_remote_copy(
            src_ref=mine,
            dst_ref=slab_sums.at[i],
            send_sem=slab_send.at[o],
            recv_sem=slab_recv.at[o],
            device_id=(lax.rem(i + o, slabs), d),
            device_id_type=MESH,
        )
        copy.start()
        sums.append(copy)
    for q, o, copy in copies:
        s = lax.rem(d + bands - o, bands)
        pltpu.make_async_remote_copy(
            src_ref=x_ref.at[0],
            dst_ref=got.at[q * bands + s],
            send_sem=send_sem.at[q * bands + o],
            recv_sem=recv_sem.at[q * bands + o],
            device_id=(i, lax.rem(d + 1, bands)),
            device_id_type=MESH,
        ).wait_recv()
        copy.wait_send()
    for e in range(bands):
        f = (e + 1) % bands
        value = got[e, 1].astype(F32) + got[f, 0].astype(F32)
        value = value + got[bands + e, 1].astype(F32) + got[bands + f, 0].astype(F32)
        slots = out_ref.shape[1]
        value = jnp.concatenate(
            [value[j * slots : (j + 1) * slots] for j in range(TILE // slots)], axis=1
        )
        out_ref[e] = value.astype(BF16)
    for o, copy in enumerate(sums, 1):
        s = lax.rem(i + slabs - o, slabs)
        pltpu.make_async_remote_copy(
            src_ref=mine,
            dst_ref=slab_sums.at[s],
            send_sem=slab_send.at[o],
            recv_sem=slab_recv.at[o],
            device_id=(lax.rem(i + 1, slabs), d),
            device_id_type=MESH,
        ).wait_recv()
        copy.wait_send()
    total = slab_sums[0]
    for s in range(1, slabs):
        total = total + slab_sums[s]
    total = total * grad_scale
    for j in range(total.shape[0]):
        total_ref[:, j * LANES : (j + 1) * LANES] = total[j : j + 1]


def block_kernel(
    slots, grid, slabs, bands,
    slot_ref, shift_ref, visible_ref, mask_ref,
    w_qkv_hbm, w_out_hbm, w_head_hbm, own_ref,
    picked_ref, sum_ref,
    joined, pix, probs, mixed, d_qkv, w_qkv_ref, w_out_ref, w_head_ref, sems,
    got_ref, x_ref, send_sem, recv_sem, halo_send, halo_recv,
):
    frames, rows, columns = grid
    groups = columns // WW
    tokens = frames * rows * columns
    width = mask_ref.shape[0]
    head_dim = width // HEADS
    parts = TILE // slots
    chunk = width // parts
    total_rows = 2 * bands * 2 * TILE
    rim_t, rim_h = WT - 1, WH - 1

    loads = [
        pltpu.make_async_copy(source, target, sems.at[m])
        for m, (source, target) in enumerate(
            (
                (w_qkv_hbm, w_qkv_ref),
                (w_out_hbm, w_out_ref),
                (own_ref, joined.at[pl.ds(rim_t, frames), pl.ds(rim_h, rows)]),
                (w_head_hbm, w_head_ref),
            )
        )
    ]
    for load in loads:
        load.start()
    halos = exchange(
        slabs, bands, slot_ref, visible_ref, own_ref, got_ref, joined,
        x_ref, send_sem, recv_sem, halo_send, halo_recv,
    )

    n = lax.broadcasted_iota(jnp.int32, (1, tokens), 1)
    group = n // (WW * WH * WT) % groups
    t_shift = h_shift = jnp.zeros((1, tokens), jnp.int32)
    for a in range(groups):
        t_shift = jnp.where(group == a, shift_ref[0, a], t_shift)
        h_shift = jnp.where(group == a, shift_ref[1, a], h_shift)
    per_pair = WW * WH * WT * groups
    t = n // (per_pair * (rows // WH)) * WT + n // (WW * WH) % WT - t_shift
    h = n // per_pair % (rows // WH) * WH + n // WW % WH - h_shift
    local = jnp.where(t < 0, t + frames, t) * rows + jnp.where(h < 0, h + rows, h)
    local = local * columns + group * WW + n % WW
    lines = [
        jnp.where(((t < 0) == (q == 1)) & ((h < 0) == (k == 0)), local, -2).astype(F32)
        for q in range(2)
        for k in range(2)
    ]
    quarter = width // 4
    rest = (width - quarter) // 2
    i, d = lax.axis_index("tm"), lax.axis_index("row")
    t_count, h_count = frames * slabs, rows * bands

    def table(count, total, base, shifts, channels):
        row = lax.broadcasted_iota(jnp.int32, (groups * count, channels), 0)
        at = base + row % count + total
        for a in range(groups):
            at = jnp.where(row // count == a, at - shift_ref[shifts, a], at)
        at = jnp.where(at >= total, at - total, at)
        return sinusoid(at.astype(F32), channels)

    pos_t = table(frames, t_count, i * frames, 0, quarter)
    pos_h = table(rows, h_count, d * rows, 1, rest)
    last = width - quarter - rest
    pos_c = sinusoid(lax.broadcasted_iota(jnp.int32, (columns, last), 0).astype(F32), last)

    received = got_ref[...].reshape(total_rows, chunk + LANES)
    index = received[:, chunk:].astype(F32)
    index = jnp.concatenate([index] * (tokens // LANES), axis=1)
    pieces = []
    for block in range(total_rows // TILE):
        q = block // (total_rows // TILE // 2)
        line = lines[2 * q + block % 2]
        pieces.append(jnp.broadcast_to(line, (TILE, tokens)))
    hit = (index == jnp.concatenate(pieces, axis=0)).astype(F32)
    part_of = lax.broadcasted_iota(jnp.int32, (total_rows, tokens), 0) // slots % parts
    part_of_t = lax.broadcasted_iota(jnp.int32, (tokens, total_rows), 1) // slots % parts
    hit_t = hit.T
    seen = jnp.max(hit_t, axis=1, keepdims=True)
    masked = 1.0 - seen
    packed_rows = received[:, :chunk]
    start = jnp.concatenate(
        [
            nn_dot(jnp.where(part_of_t == j, hit_t, 0.0).astype(BF16), packed_rows)
            for j in range(parts)
        ],
        axis=1,
    )
    start = jnp.where(seen > 0, start, mask_ref[...].astype(F32)[None, :])

    order = [
        (fw, hw, g, ft, r)
        for fw in range(frames // WT)
        for hw in range(rows // WH)
        for g in range(groups)
        for ft in range(WT)
        for r in range(WH)
    ]
    pieces = []
    for fw, hw, g, ft, r in order:
        t_line = g * frames + fw * WT + ft
        h_line = g * rows + hw * WH + r
        pieces.append(
            jnp.concatenate(
                [
                    jnp.broadcast_to(pos_t[t_line : t_line + 1], (WW, quarter)),
                    jnp.broadcast_to(pos_h[h_line : h_line + 1], (WW, rest)),
                    pos_c[g * WW : (g + 1) * WW],
                ],
                axis=1,
            )
        )
    embedded = (start + jnp.concatenate(pieces, axis=0)).astype(BF16).astype(F32)

    normed, scale = norm_parts(embedded)
    loads[0].wait()
    qkv = nn_dot(normed.astype(BF16), w_qkv_ref[...]).astype(BF16)

    window = WT * WH * WW
    span = 2 * window
    pair = 2 * head_dim
    same = (
        lax.broadcasted_iota(jnp.int32, (span, span), 0) // window
        == lax.broadcasted_iota(jnp.int32, (span, span), 1) // window
    )
    lane = lax.broadcasted_iota(jnp.int32, (span, pair), 1) // head_dim
    zero = jnp.zeros((span, pair), BF16)

    def halves(values):
        return jnp.concatenate(
            [jnp.where(lane == 0, values, zero), jnp.where(lane == 1, values, zero)], axis=0
        )

    def block_of(values, b, at):
        return values[b * span : (b + 1) * span, at : at + pair]

    for b in range(tokens // span):
        for p in range(HEADS // 2):
            q = block_of(qkv, b, p * pair)
            k = block_of(qkv, b, width + p * pair)
            v = block_of(qkv, b, 2 * width + p * pair)
            scores = nt_dot(q, halves(k)) * head_dim ** (-0.5)
            both = []
            for m in range(2):
                part = jnp.where(same, scores[:, m * span : (m + 1) * span], -jnp.inf)
                weights = jnp.exp(part - jnp.max(part, axis=-1, keepdims=True))
                both.append(weights * (1.0 / jnp.sum(weights, axis=-1, keepdims=True)))
            weights = jnp.concatenate(both, axis=1)
            probs[b * HEADS // 2 + p] = weights
            out = nn_dot(weights.astype(BF16), halves(v))
            mixed[b * span : (b + 1) * span, p * pair : (p + 1) * pair] = out.astype(BF16)
    loads[1].wait()
    attn = nn_dot(mixed[...], w_out_ref[...]).astype(BF16)
    residual = embedded + attn.astype(F32)

    loads[2].wait()
    for copy in halos:
        copy.wait()
    for n, (fw, hw, g, ft, r) in enumerate(order):
        t = fw * WT + ft + rim_t - shift_ref[0, g]
        h = hw * WH + r + rim_h - shift_ref[1, g]
        pix[n * WW : (n + 1) * WW, :] = joined[t, h][
            g * WW : (g + 1) * WW, :
        ].astype(F32)
    group_size = pix.shape[1] // 3
    targets = []
    for c in range(3):
        raw = pix[:, c * group_size : (c + 1) * group_size]
        center = raw - jnp.mean(raw, axis=-1, keepdims=True)
        spread = jnp.sqrt(jnp.sum(center * center, axis=-1, keepdims=True) / (group_size - 1))
        targets.append(center * (1.0 / (spread + 1e-06)))
    target = jnp.concatenate(targets, axis=1)

    normed_out, scale_out = norm_parts(residual)
    loads[3].wait()
    predicted = nn_dot(normed_out.astype(BF16), w_head_ref[...])
    errors = (predicted - target) * masked
    d_normed_out = nt_dot(errors.astype(BF16), w_head_ref[...]).astype(BF16).astype(F32)
    grad_residual = norm_grad(d_normed_out, normed_out, scale_out)
    d_mixed = nt_dot(grad_residual.astype(BF16), w_out_ref[...]).astype(BF16)

    for b in range(tokens // span):
        for p in range(HEADS // 2):
            q = block_of(qkv, b, p * pair)
            k = block_of(qkv, b, width + p * pair)
            v = block_of(qkv, b, 2 * width + p * pair)
            d_out = block_of(d_mixed, b, p * pair)
            weights = probs[b * HEADS // 2 + p]
            d_weights = nt_dot(d_out, halves(v)).astype(BF16).astype(F32)
            both = []
            for m in range(2):
                w = weights[:, m * span : (m + 1) * span]
                dw = d_weights[:, m * span : (m + 1) * span]
                inner = jnp.sum(w * dw, axis=-1, keepdims=True)
                both.append(w * (dw - inner) * head_dim ** (-0.5))
            d_scores = jnp.concatenate(both, axis=1).astype(BF16)
            dq = nn_dot(d_scores, halves(k))
            dk = tn_dot(d_scores, q)
            dv = tn_dot(weights.astype(BF16), d_out)
            dk = jnp.where(lane == 0, dk[:span], dk[span:])
            dv = jnp.where(lane == 0, dv[:span], dv[span:])
            for m, value in enumerate((dq, dk, dv)):
                at = m * width + p * pair
                d_qkv[b * span : (b + 1) * span, at : at + pair] = value.astype(BF16)
    d_normed = nt_dot(d_qkv[...], w_qkv_ref[...]).astype(BF16).astype(F32)
    grad = grad_residual + norm_grad(d_normed, normed, scale)

    line = jnp.sum(grad * masked, axis=0, keepdims=True)
    for j in range(width // LANES):
        sum_ref[j : j + 1, :] = line[:, j * LANES : (j + 1) * LANES]
    rounded = grad.astype(BF16)
    picked = None
    for j in range(parts):
        term = nn_dot(
            jnp.where(part_of == j, hit, 0.0).astype(BF16), rounded[:, j * chunk : (j + 1) * chunk]
        )
        picked = term if picked is None else picked + term
    picked_ref[...] = picked.astype(BF16)


def per_device(visible, slot_pos, window_shift, mask_token, w_qkv, w_out, w_head, pixels):
    frames, rows, columns, pixel_count = pixels.shape
    width = mask_token.shape[0]
    tokens = frames * rows * columns
    bands, slots = slot_pos.shape[2:]
    slabs = lax.axis_size("tm")
    parts = TILE // slots
    chunk = width // parts
    rim_t, rim_h = WT - 1, WH - 1
    vmem = pl.BlockSpec(memory_space=pltpu.VMEM)
    smem = pl.BlockSpec(memory_space=pltpu.SMEM)
    anywhere = pl.BlockSpec(memory_space=pl.ANY)
    wide = chunk + LANES
    total_rows = 2 * bands * 2 * TILE
    flops = 4 * tokens * width * (w_qkv.shape[1] + width + pixel_count)
    picked, partial_sum = pl.pallas_call(
        functools.partial(block_kernel, slots, (frames, rows, columns), slabs, bands),
        out_shape=(
            jax.ShapeDtypeStruct((total_rows, chunk), BF16),
            jax.ShapeDtypeStruct((width // LANES, LANES), F32),
        ),
        in_specs=[smem, smem, vmem, vmem] + [anywhere] * 4,
        out_specs=(vmem, vmem),
        scratch_shapes=[
            pltpu.VMEM((frames + rim_t, rows + rim_h, columns, pixel_count), BF16),
            pltpu.VMEM((tokens, pixel_count), F32),
            pltpu.VMEM(
                (HEADS * tokens // (4 * WT * WH * WW), 2 * WT * WH * WW, 4 * WT * WH * WW), F32
            ),
            pltpu.VMEM((tokens, width), BF16),
            pltpu.VMEM((tokens, 3 * width), BF16),
            pltpu.VMEM(w_qkv.shape, BF16),
            pltpu.VMEM(w_out.shape, BF16),
            pltpu.VMEM(w_head.shape, BF16),
            pltpu.SemaphoreType.DMA((4,)),
            pltpu.VMEM((2 * bands, 2, TILE, wide), BF16),
            pltpu.VMEM((bands, 2, TILE, wide), BF16),
            pltpu.SemaphoreType.DMA((2 * bands,)),
            pltpu.SemaphoreType.DMA((2 * bands,)),
            pltpu.SemaphoreType.DMA((3,)),
            pltpu.SemaphoreType.DMA((3,)),
        ],
        compiler_params=pltpu.CompilerParams(
            collective_id=0, has_side_effects=True, vmem_limit_bytes=56 * 2**20
        ),
        cost_estimate=pl.CostEstimate(
            flops=flops, bytes_accessed=16 * 2**20, transcendentals=HEADS * tokens * 128
        ),
        name="block",
    )(
        slot_pos, window_shift, visible, mask_token, w_qkv, w_out, w_head, pixels,
    )

    lines = width // LANES
    returned, total = pl.pallas_call(
        functools.partial(collect_kernel, slabs, bands, (tokens * slabs * bands) ** (-0.5)),
        out_shape=(
            jax.ShapeDtypeStruct((bands, slots, width), BF16),
            jax.ShapeDtypeStruct((1, width), F32),
        ),
        in_specs=[vmem, vmem],
        out_specs=(vmem, vmem),
        scratch_shapes=[
            pltpu.VMEM((2 * bands, 2, TILE, chunk), BF16),
            pltpu.VMEM((bands, lines, LANES), F32),
            pltpu.VMEM((slabs, lines, LANES), F32),
            pltpu.VMEM((lines, LANES), F32),
            pltpu.SemaphoreType.DMA((2 * bands,)),
            pltpu.SemaphoreType.DMA((2 * bands,)),
            pltpu.SemaphoreType.DMA((bands,)),
            pltpu.SemaphoreType.DMA((bands,)),
            pltpu.SemaphoreType.DMA((slabs,)),
            pltpu.SemaphoreType.DMA((slabs,)),
        ],
        compiler_params=pltpu.CompilerParams(collective_id=1, has_side_effects=True),
        name="collect",
    )(picked.reshape(2 * bands, 2, TILE, chunk), partial_sum)
    return returned.reshape(visible.shape), total.reshape(width)


def solution(mesh):
    placed = (
        P("tm", "row", None, None, None),
        P("tm", "row", None, None),
        P(),
        P(),
        P(),
        P(),
        P(),
        P("tm", "row", None, None),
    )
    return jax.shard_map(
        per_device,
        mesh=mesh,
        in_specs=placed,
        out_specs=(P("tm", "row", None, None, None), P()),
        check_vma=False,
    )
```
